512 devices in a mesh: dp: 32 (over x, y), seq: 16 (over z, core).
Axes of the slice: x: 4, y: 8, z: 8, core: 2. Of those that a mesh axis runs over, the one named last changes fastest.
Arguments:
- frames: bfloat16 [32, 2048, 1536], P('dp', 'seq'), may hold values from -6 to 6
- lengths: int32 [32], P('dp'), may hold values from 512 to 2048, as said below
- w_qkv: bfloat16 [1536, 16, 288], P(None, 'seq'), may hold values from -1 to 1
- w_out: bfloat16 [16, 96, 1536], P('seq'), may hold values from -0.15625 to 0.15625
- kernel: bfloat16 [9, 1536], replicated, may hold values from -2 to 2
- bn_scale: float32 [1536], replicated, may hold values from 0.5 to 2
- bn_shift: float32 [1536], replicated, may hold values from -3 to 3
- cotangent: bfloat16 [32, 2048, 1536], P('dp', 'seq'), may hold values from -6 to 6
Outputs:
- layer_out: bfloat16 [32, 2048, 1536], P('dp', 'seq')
- grad_qkv: float32 [1536, 16, 288], P('dp', 'seq')
- grad_kernel: float32 [9, 1536], replicated
- grad_scale: float32 [1536], replicated
- grad_shift: float32 [1536], replicated
The draws below stay inside these ranges and needn't reach their ends.
Inputs may be any that keep to these rules, and one draw needn't show every extreme that they name: `lengths`: some recording has exactly 2048 valid frames in every draw.
All inputs are finite; a program needn't handle non-finite values.
Results may differ from the reference program's by a relative error of at most 0.012.
Values may be sent and summed in bfloat16 or wider, within the bound.
No kernel may reach another device: no remote copies, remote signals or barrier semaphores. Data moves between devices by JAX's collectives and lax.ppermute only.
A program may use at most 64 MiB of HBM per device.

```python
import math
import jax
import jax.numpy as jnp
from jax import lax

D = 1536
HD = 96
KERNEL = 9
WIN = 128
HEADS = 16
ATT = 1536
SEQ_LEN = 2048
RECS = 32
REACH = 4


def draw_lengths(key, part):
    key = jax.random.fold_in(key, 7)
    first_key, second_key = jax.random.split(key)
    drawn = jax.random.randint(first_key, (RECS,), SEQ_LEN // 4, SEQ_LEN + 1)
    chosen = jax.random.randint(second_key, (), 0, RECS)
    return jnp.where(jnp.arange(RECS) == chosen, SEQ_LEN, drawn).astype(jnp.int32)


def draw_w_qkv(key, part):
    key = jax.random.fold_in(key, 11)
    first_key, second_key, third_key = jax.random.split(key, 3)
    array_shape = (D, HEADS, HD)
    factor = D ** (-0.5)
    shared = jax.random.normal(first_key, array_shape, jnp.float32)
    other = jax.random.normal(second_key, array_shape, jnp.float32)
    value_part = jax.random.normal(third_key, array_shape, jnp.float32) * factor
    query_part = shared * factor
    key_part = other * factor
    return jnp.clip(jnp.concatenate([query_part, key_part, value_part], axis=-1), -1.0, 1.0).astype(jnp.bfloat16)


def steps_of(own_key, dims, cuts, least, high):
    factor_of, own = 1.0, jax.random.fold_in(own_key, 6)
    for position, shards_of in cuts:
        heights = jnp.exp(jax.random.uniform(jax.random.fold_in(own, position), (shards_of,), jnp.float32, least / len(cuts), high / len(cuts)))
        factor_of = factor_of * jnp.repeat(heights, dims[position] // shards_of).reshape([-1 if axis == position else 1 for axis in range(len(dims))])
    return factor_of


def normal_values(own_key, dims, scale, reach, pieces=(), kind=jnp.bfloat16):
    factor_of = steps_of(own_key, dims, pieces, -0.22, 0.18) if pieces else 1.0
    result = jax.random.normal(own_key, dims, jnp.float32) * scale * factor_of
    return jnp.minimum(jnp.maximum(result, -reach), reach).astype(kind)


def setup_inputs(seed: int = 0) -> dict:
    key_of = jax.random.split(jax.random.key(seed), 9)
    frames = normal_values(key_of[0], (RECS, SEQ_LEN, D), 1.0, 6.0, ((0, 32), (1, 16)))
    lengths = draw_lengths(jax.random.fold_in(key_of[8], 71), 0)
    w_qkv = draw_w_qkv(jax.random.fold_in(key_of[8], 71), 0)
    w_out = normal_values(key_of[3], (HEADS, HD, D), ATT ** -0.5, 0.15625, ((0, 16),))
    kernel = normal_values(key_of[4], (KERNEL, D), KERNEL ** -0.5, 2.0)
    bn_scale = jnp.clip(jnp.exp(jax.random.uniform(key_of[5], (D,), jnp.float32, math.log(0.5), math.log(2.0))), 0.5, 2.0)
    bn_shift = normal_values(key_of[6], (D,), 0.5, 3.0, (), jnp.float32)
    cotangent = normal_values(key_of[7], (RECS, SEQ_LEN, D), 1.0, 6.0, ((0, 32), (1, 16)))
    return {"frames": frames, "lengths": lengths, "w_qkv": w_qkv, "w_out": w_out, "kernel": kernel, "bn_scale": bn_scale, "bn_shift": bn_shift, "cotangent": cotangent}


EPS = 1e-05
FLOOR = 1.0

def layer_norm(rows):
    values = rows.astype(jnp.float32)
    center = values - lax.optimization_barrier(jnp.mean(values, axis=-1, keepdims=True))
    spread = lax.optimization_barrier(jnp.mean(center * center, axis=-1, keepdims=True))
    return (center * lax.rsqrt(spread + EPS)).astype(jnp.bfloat16)

def band_keys(key_rows, attention_radius_width):
    segment_count = key_rows.shape[0] // attention_radius_width
    blocks = key_rows.reshape(segment_count, attention_radius_width, key_rows.shape[-1])
    padded = jnp.pad(blocks, ((1, 1), (0, 0), (0, 0)))
    return jnp.concatenate([padded[:-2], padded[1:-1], padded[2:]], axis=1)

def fold_stripe(band, attention_radius_width):
    segment_count = band.shape[0]
    parts = band.reshape(segment_count, 3, attention_radius_width, band.shape[-1])
    padded = jnp.pad(parts, ((1, 1), (0, 0), (0, 0), (0, 0)))
    folded = padded[2:, 0] + padded[1:-1, 1] + padded[:-2, 2]
    return folded.reshape(segment_count * attention_radius_width, band.shape[-1])

def band_mask(segment_count, attention_radius_width, length):
    row_pos = jnp.arange(attention_radius_width, dtype=jnp.int32)[:, None]
    col_pos = jnp.arange(3 * attention_radius_width, dtype=jnp.int32)[None, :]
    nearby = jnp.abs(row_pos + attention_radius_width - col_pos) <= attention_radius_width
    key_pos = jnp.arange(segment_count, dtype=jnp.int32)[:, None, None] * attention_radius_width - attention_radius_width + col_pos[None]
    return nearby[None] & (key_pos >= 0) & (key_pos < length)

def attend_forward(query_lines, key_rows, value_rows, mask):
    segment_count, attention_radius_width = (mask.shape[0], mask.shape[1])
    query_tiles = query_lines.reshape(segment_count, attention_radius_width, -1).astype(jnp.float32)
    neighbour_lookup_rows = band_keys(key_rows, attention_radius_width).astype(jnp.float32)
    neighbour_content_rows = band_keys(value_rows, attention_radius_width).astype(jnp.float32)
    logit_scores = jnp.einsum('oaz,ofz->oaf', query_tiles, neighbour_lookup_rows) * query_lines.shape[-1] ** (-0.5)
    logit_scores = jnp.where(mask, logit_scores, -1e+30)
    top_score = lax.optimization_barrier(jnp.max(logit_scores, axis=-1, keepdims=True))
    exponent = jnp.where(mask, jnp.exp(logit_scores - top_score), 0.0)
    denominator = jnp.maximum(lax.optimization_barrier(jnp.sum(exponent, axis=-1, keepdims=True)), FLOOR)
    normalized_probabilities = (exponent / denominator).astype(jnp.bfloat16)
    mixed_attention_result = jnp.einsum('mnb,mbo->mno', normalized_probabilities.astype(jnp.float32), neighbour_content_rows)
    return (mixed_attention_result.reshape(segment_count * attention_radius_width, -1), normalized_probabilities)

def attend_backward(query_lines, key_rows, value_rows, normalized_probabilities, grad_rows, mask):
    segment_count, attention_radius_width = (mask.shape[0], mask.shape[1])
    head_dim = query_lines.shape[-1]
    query_tiles = query_lines.reshape(segment_count, attention_radius_width, -1).astype(jnp.float32)
    neighbour_lookup_rows = band_keys(key_rows, attention_radius_width).astype(jnp.float32)
    neighbour_content_rows = band_keys(value_rows, attention_radius_width).astype(jnp.float32)
    block_gradients = grad_rows.reshape(segment_count, attention_radius_width, -1).astype(jnp.float32)
    softmax_broad = normalized_probabilities.astype(jnp.float32)
    value_gradient = fold_stripe(jnp.einsum('ovj,ovp->ojp', softmax_broad, block_gradients), attention_radius_width)
    softmax_gradient = jnp.einsum('oaz,ofz->oaf', block_gradients, neighbour_content_rows)
    inner = lax.optimization_barrier(jnp.sum(softmax_broad * softmax_gradient, axis=-1, keepdims=True))
    affinity_cotangent = (softmax_broad * (softmax_gradient - inner) * head_dim ** (-0.5)).astype(jnp.bfloat16).astype(jnp.float32)
    request_cotangent = jnp.einsum('mnb,mbo->mno', affinity_cotangent, neighbour_lookup_rows).reshape(segment_count * attention_radius_width, -1)
    key_gradient = fold_stripe(jnp.einsum('ovj,ovp->ojp', affinity_cotangent, query_tiles), attention_radius_width)
    return jnp.concatenate([request_cotangent, key_gradient, value_gradient], axis=-1).astype(jnp.bfloat16)

def one_recording(frame_rows, length, w_qkv, w_out, kernel, bn_scale, bn_shift, grad_out):
    live_rows = (jnp.arange(SEQ_LEN, dtype=jnp.int32) < length)[:, None]
    normed = layer_norm(frame_rows)
    qkv_rows = jnp.dot(normed, w_qkv.reshape(D, HEADS * 3 * HD), preferred_element_type=jnp.float32)
    qkv_rows = qkv_rows.astype(jnp.bfloat16).reshape(SEQ_LEN, HEADS, 3 * HD)
    query_lines = qkv_rows[:, :, :HD]
    key_rows = qkv_rows[:, :, HD:2 * HD]
    value_rows = qkv_rows[:, :, 2 * HD:]
    mask = band_mask(SEQ_LEN // WIN, WIN, length)
    mixed_attention_result, normalized_probabilities = jax.vmap(attend_forward, in_axes=(1, 1, 1, None), out_axes=(1, 0))(query_lines, key_rows, value_rows, mask)
    mixed_attention_result = jnp.where(live_rows[:, :, None], mixed_attention_result, 0.0).astype(jnp.bfloat16).reshape(SEQ_LEN, ATT)
    out_matrix = w_out.reshape(ATT, D)
    attended = jnp.dot(mixed_attention_result, out_matrix, preferred_element_type=jnp.float32)
    hidden = (frame_rows.astype(jnp.float32) + attended).astype(jnp.bfloat16)
    masked = jnp.where(live_rows, hidden, jnp.zeros_like(hidden))
    padded = jnp.pad(masked.astype(jnp.float32), ((REACH, REACH), (0, 0)))
    taps = kernel.astype(jnp.float32)
    conv = jnp.zeros((SEQ_LEN, D), jnp.float32)
    for offset in range(KERNEL):
        conv = conv + padded[offset:offset + SEQ_LEN] * taps[offset]
    shifted = conv * bn_scale + bn_shift
    layer_out = (hidden.astype(jnp.float32) + jax.nn.silu(shifted)).astype(jnp.bfloat16)
    upstream = grad_out.astype(jnp.float32)
    sigmoid_val = jax.nn.sigmoid(shifted)
    d_shifted = upstream * sigmoid_val * (1.0 + shifted * (1.0 - sigmoid_val))
    grad_shift = lax.optimization_barrier(jnp.sum(d_shifted, axis=0))
    grad_scale = lax.optimization_barrier(jnp.sum(d_shifted * conv, axis=0))
    d_conv = d_shifted * bn_scale
    grad_kernel = jnp.stack([lax.optimization_barrier(jnp.sum(d_conv * padded[offset:offset + SEQ_LEN], axis=0)) for offset in range(KERNEL)])
    d_padded = jnp.pad(d_conv, ((REACH, REACH), (0, 0)))
    spread = jnp.zeros((SEQ_LEN, D), jnp.float32)
    for offset in range(KERNEL):
        spread = spread + taps[offset] * d_padded[2 * REACH - offset:2 * REACH - offset + SEQ_LEN]
    d_hidden = (upstream + jnp.where(live_rows, spread, 0.0)).astype(jnp.bfloat16)
    d_mixed = jnp.dot(d_hidden, out_matrix.T, preferred_element_type=jnp.float32)
    d_mixed = jnp.where(live_rows, d_mixed, 0.0).astype(jnp.bfloat16).reshape(SEQ_LEN, HEADS, HD)
    d_qkv = jax.vmap(attend_backward, in_axes=(1, 1, 1, 0, 1, None), out_axes=1)(query_lines, key_rows, value_rows, normalized_probabilities, d_mixed, mask)
    grad_qkv = jnp.dot(normed.T, d_qkv.reshape(SEQ_LEN, HEADS * 3 * HD), preferred_element_type=jnp.float32)
    return (layer_out, grad_qkv.reshape(D, HEADS, 3 * HD), grad_kernel, grad_scale, grad_shift)

def reference(frames, lengths, w_qkv, w_out, kernel, bn_scale, bn_shift, cotangent):

    def advance(carry_sums, record):
        frame_rows, length, grad_out = record
        layer_out, grad_qkv, grad_kernel, grad_scale, grad_shift = one_recording(frame_rows, length, w_qkv, w_out, kernel, bn_scale, bn_shift, grad_out)
        updated = (carry_sums[0] + grad_qkv, carry_sums[1] + grad_kernel, carry_sums[2] + grad_scale, carry_sums[3] + grad_shift)
        return (updated, layer_out)
    initial = (jnp.zeros((D, HEADS, 3 * HD), jnp.float32), jnp.zeros((KERNEL, D), jnp.float32), jnp.zeros((D,), jnp.float32), jnp.zeros((D,), jnp.float32))
    totals, outputs = lax.scan(advance, initial, (frames, lengths, cotangent))
    return (outputs, totals[0], totals[1], totals[2], totals[3])
```

```python
import functools

import jax
import jax.numpy as jnp
from jax import lax
from jax.experimental import pallas as pl
from jax.experimental.pallas import tpu as pltpu
from jax.sharding import PartitionSpec as P

WIN = 128
EPS = 1e-05
FLOOR = 1.0
EDGE = 8
LANES = 128
F32 = jnp.float32
BF16 = jnp.bfloat16

VMEM = pl.BlockSpec(memory_space=pltpu.VMEM)
SMEM = pl.BlockSpec(memory_space=pltpu.SMEM)
ANYWHERE = pl.BlockSpec(memory_space=pl.ANY)


def params(mib):
    return pltpu.CompilerParams(vmem_limit_bytes=mib * 1024 * 1024)


def dot(a, b, dims):
    return lax.dot_general(a, b, ((dims[:1], dims[1:]), ((), ())), preferred_element_type=F32)


def norm_kernel(x_ref, w_ref, packed_ref):
    rows = x_ref.shape[0]
    values = x_ref[...].astype(F32)
    center = values - jnp.mean(values, axis=-1, keepdims=True)
    spread = jnp.mean(center * center, axis=-1, keepdims=True)
    packed_ref[0:rows, :] = (center * lax.rsqrt(spread + EPS)).astype(BF16)
    packed_ref[rows:, :] = w_ref[...]


def forward_kernel(
    len_ref, packed_ref, wt_ref, out_ref, qkvt_ref, k_ref, v_ref, soft_ref, normed, mixed, sems
):
    blocks = packed_ref.shape[0]
    hd = k_ref.shape[1]
    total = blocks * WIN
    per = blocks // sems.shape[0]
    copies = [
        pltpu.make_async_copy(
            packed_ref.at[pl.ds(c * per, per), pl.ds(0, WIN), :],
            normed.at[pl.ds(c * per, per)],
            sems.at[c],
        )
        for c in range(sems.shape[0])
    ]
    for copy in copies:
        copy.start()
    length = len_ref[0]
    for edge in (slice(0, WIN), slice(WIN + total, 2 * WIN + total)):
        qkvt_ref[:, edge] = jnp.zeros((3 * hd, WIN), BF16)
        k_ref[edge, :] = jnp.zeros((WIN, hd), BF16)
        v_ref[edge, :] = jnp.zeros((WIN, hd), BF16)
    mixed[0] = jnp.zeros(mixed.shape[1:], F32)
    mixed[blocks + 1] = jnp.zeros(mixed.shape[1:], F32)
    wt = wt_ref[...]
    for c, copy in enumerate(copies):
        copy.wait()
        rows = normed[c * per : (c + 1) * per].reshape(per * WIN, normed.shape[2])
        part = dot(wt, rows, (1, 1))
        at = slice(WIN + c * per * WIN, WIN + (c + 1) * per * WIN)
        qkvt_ref[:, at] = part.astype(BF16)
        k_ref[at, :] = part[hd : 2 * hd].T.astype(BF16)
        v_ref[at, :] = part[2 * hd :].T.astype(BF16)

    key = lax.broadcasted_iota(jnp.int32, (3 * WIN, WIN), 0)
    query = lax.broadcasted_iota(jnp.int32, (3 * WIN, WIN), 1)
    near = (key >= query) & (key - query <= 2 * WIN)
    column = lax.broadcasted_iota(jnp.int32, (1, WIN), 1)
    scale = hd ** (-0.5)

    def attend(i, carry):
        start = pl.multiple_of(i * WIN, WIN)
        q = qkvt_ref[0:hd, pl.ds(pl.multiple_of(start + WIN, WIN), WIN)]
        key_pos = key + (start - WIN)
        mask = near & (key_pos >= 0) & (key_pos < length)
        scores = dot(k_ref[pl.ds(start, 3 * WIN), :], q, (1, 0)) * scale
        scores = jnp.where(mask, scores, -1e30)
        top = jnp.max(scores, axis=0, keepdims=True)
        expo = jnp.where(mask, jnp.exp(scores - top), 0.0)
        denominator = jnp.maximum(jnp.sum(expo, axis=0, keepdims=True), FLOOR)
        soft = (expo * (1.0 / denominator)).astype(BF16)
        soft_ref[i] = soft
        result = dot(qkvt_ref[2 * hd : 3 * hd, pl.ds(start, 3 * WIN)], soft, (1, 0))
        result = jnp.where(column + start < length, result, 0.0)
        mixed[i + 1, 0:hd, :] = result
        mixed[i + 1, hd:, :] = jnp.zeros((mixed.shape[1] - hd, WIN), F32)
        out_ref[i, 0:hd, :] = result.astype(BF16)
        return carry

    lax.fori_loop(0, blocks, attend, 0, unroll=4)

    def edges(i, carry):
        both = jnp.where(column < EDGE, mixed[i + 2], mixed[i]).T
        rows = jnp.concatenate([both[WIN - EDGE :], both[:EDGE]], axis=0)
        out_ref[i, hd:, :] = rows.astype(BF16)
        return carry

    lax.fori_loop(0, blocks, edges, 0, unroll=4)


def middle_kernel(
    chunk, total, place_ref, mix_ref, packed_ref, x_ref, g_ref, prev_ref, next_ref, taps_ref,
    scale_ref, shift_ref, layer_ref, out_ref, weight, d_hidden, masked, d_conv, small, sem
):
    heads, width = mix_ref.shape[0], x_ref.shape[1]
    rows = x_ref.shape[0]
    hd = weight.shape[1]
    taps_count = taps_ref.shape[0]
    reach = (taps_count - 1) // 2
    ext = rows + 2 * EDGE
    copy = pltpu.make_async_copy(packed_ref.at[:, pl.ds(rows, hd), :], weight, sem)
    copy.start()
    base, length = place_ref[0], place_ref[1]
    body = mix_ref[:, 0:hd, :].reshape(heads * hd, rows).T
    fringe = jnp.concatenate([mix_ref[h, hd:, 0:hd] for h in range(heads)], axis=1)
    mix = jnp.concatenate([body, fringe], axis=0)
    pos = lax.broadcasted_iota(jnp.int32, (ext, 1), 0) + (base - EDGE)
    live = (pos >= 0) & (pos < length)
    inside = (pos >= 0) & (pos < total)
    live_here = live[EDGE : EDGE + rows]
    small[...] = jnp.zeros(small.shape, F32)
    masked[0:reach, :] = jnp.zeros((reach, chunk), F32)
    masked[reach + ext :, :] = jnp.zeros((reach, chunk), F32)
    copy.wait()
    for c in range(width // chunk):
        at = slice(c * chunk, (c + 1) * chunk)
        w = weight[:, :, at].reshape(heads * hd, chunk)
        attended = dot(mix, w, (1, 0))
        attended = jnp.concatenate(
            [attended[rows : rows + EDGE], attended[:rows], attended[rows + EDGE :]], axis=0
        )
        before = prev_ref[:, at].astype(F32)
        after = next_ref[:, at].astype(F32)
        frames = jnp.concatenate([before[:EDGE], x_ref[:, at].astype(F32), after[:EDGE]], axis=0)
        upstream = jnp.concatenate([before[EDGE:], g_ref[:, at].astype(F32), after[EDGE:]], axis=0)
        hidden = (frames + attended).astype(BF16).astype(F32)
        masked[reach : reach + ext, :] = jnp.where(live, hidden, 0.0)
        taps = taps_ref[:, at].astype(F32)
        conv = jnp.zeros((ext, chunk), F32)
        for k in range(taps_count):
            conv = conv + masked[k : k + ext, :] * taps[k : k + 1]
        gain = scale_ref[:, at]
        shifted = conv * gain + shift_ref[:, at]
        sigmoid = jax.nn.sigmoid(shifted)
        d_shifted = upstream * sigmoid * (1.0 + shifted * (1.0 - sigmoid))
        own = slice(EDGE, EDGE + rows)
        layer_ref[:, at] = (hidden[own] + (shifted * sigmoid)[own]).astype(BF16)
        d_own = d_shifted[own]
        small[taps_count : taps_count + 1, at] = jnp.sum(d_own * conv[own], axis=0, keepdims=True)
        small[taps_count + 1 : taps_count + 2, at] = jnp.sum(d_own, axis=0, keepdims=True)
        d_conv[...] = jnp.where(inside, d_shifted * gain, 0.0)
        d_conv_own = d_own * gain
        spread = jnp.zeros((rows, chunk), F32)
        for k in range(taps_count):
            small[k : k + 1, at] = jnp.sum(
                d_conv_own * masked[EDGE + k : EDGE + k + rows, :], axis=0, keepdims=True
            )
            first = EDGE + reach - k
            spread = spread + taps[k : k + 1] * d_conv[first : first + rows, :]
        d_hidden[:, at] = (upstream[own] + jnp.where(live_here, spread, 0.0)).astype(BF16)
    column = lax.broadcasted_iota(jnp.int32, (1, rows), 1) + base
    group = 4
    for h in range(0, heads, group):
        w = weight[h : h + group].reshape(group * hd, width)
        d_mixed = dot(w, d_hidden[...], (1, 1))
        d_mixed = jnp.where(column < length, d_mixed, 0.0).astype(BF16)
        out_ref[h : h + group, 0:hd, :] = d_mixed.reshape(group, hd, rows)
    high = small[...].astype(BF16)
    low = (small[...] - high.astype(F32)).astype(BF16)
    half = small.shape[0]
    for h in range(heads):
        if (h + 1) * LANES <= width:
            at = slice(h * LANES, (h + 1) * LANES)
            out_ref[h, hd : hd + half, :] = high[:, at]
            out_ref[h, hd + half :, :] = low[:, at]
        else:
            out_ref[h, hd:, :] = jnp.zeros((2 * half, rows), BF16)


def backward_kernel(
    shares, in_ref, packed_ref, qkvt_ref, k_ref, v_ref, soft_ref, out_ref,
    normed, d_query, d_key, d_value, joined, grad, sem
):
    blocks, width = packed_ref.shape[0], packed_ref.shape[2]
    hd = k_ref.shape[1]
    total = blocks * WIN
    copy = pltpu.make_async_copy(packed_ref.at[:, pl.ds(0, WIN), :], normed, sem)
    copy.start()
    d_key[...] = jnp.zeros(d_key.shape, F32)
    d_value[...] = jnp.zeros(d_value.shape, F32)
    scale = hd ** (-0.5)

    def attend(i, carry):
        start = pl.multiple_of(i * WIN, WIN)
        own = pl.ds(pl.multiple_of(start + WIN, WIN), WIN)
        window = pl.ds(start, 3 * WIN)
        d_mixed = in_ref[i, 0:hd, :]
        soft = soft_ref[i]
        wide = soft.astype(F32)
        d_soft = dot(v_ref[window, :], d_mixed, (1, 0))
        inner = jnp.sum(wide * d_soft, axis=0, keepdims=True)
        d_scores = (wide * (d_soft - inner) * scale).astype(BF16)
        d_query[:, pl.ds(start, WIN)] = dot(qkvt_ref[hd : 2 * hd, window], d_scores, (1, 0)).astype(BF16)
        d_key[:, window] += dot(qkvt_ref[0:hd, own], d_scores, (1, 1))
        d_value[:, window] += dot(d_mixed, soft, (1, 1))
        return carry

    lax.fori_loop(0, blocks, attend, 0, unroll=4)
    joined[0:hd, :] = d_query[...]
    joined[hd : 2 * hd, :] = d_key[:, WIN : WIN + total].astype(BF16)
    joined[2 * hd :, :] = d_value[:, WIN : WIN + total].astype(BF16)
    copy.wait()
    rest = 3 * hd - 2 * LANES
    copies = LANES // rest
    step = 512
    for c in range(width // step):
        at = slice(c * step, (c + 1) * step)
        rows = normed[:, :, at].reshape(total, step)
        part = dot(joined[...], rows, (1, 0))
        tail = part[2 * LANES :]
        grad[at, :] = jnp.concatenate([part[: 2 * LANES]] + [tail] * copies, axis=0).T
    share = width // shares
    third = share // (copies - 1)
    lane = lax.broadcasted_iota(jnp.int32, (1, LANES), 1) // rest
    half = (in_ref.shape[1] - hd) // 2
    small = jnp.sum(in_ref[:, hd : hd + half, :].astype(F32), axis=0) + jnp.sum(
        in_ref[:, hd + half :, :].astype(F32), axis=0
    )
    small = small.astype(BF16)
    for d in range(shares):
        at = slice(d * share, (d + 1) * share)
        out_ref[d, 0:share, :] = grad[at, 0:LANES].astype(BF16)
        out_ref[d, share : 2 * share, :] = grad[at, LANES : 2 * LANES].astype(BF16)
        packed = jnp.zeros((third, LANES), F32)
        for j in range(copies - 1):
            first = d * share + j * third
            packed = jnp.where(lane == j, grad[first : first + third, 2 * LANES :], packed)
        out_ref[d, 2 * share : 2 * share + third, :] = packed.astype(BF16)
        out_ref[d, 2 * share + third :, :] = small


def sum_kernel(in_ref, grad_ref, small_ref):
    share, columns = grad_ref.shape
    third = in_ref.shape[1] - 2 * share - small_ref.shape[0]
    rest = columns - 2 * LANES
    summed = jnp.sum(in_ref[...].astype(F32), axis=0)
    grad_ref[:, 0:LANES] = summed[0:share]
    grad_ref[:, LANES : 2 * LANES] = summed[share : 2 * share]
    for j in range(share // third):
        grad_ref[j * third : (j + 1) * third, 2 * LANES :] = summed[
            2 * share : 2 * share + third, j * rest : (j + 1) * rest
        ]
    small_ref[...] = summed[2 * share + third :]


def spread_kernel(in_ref, kernel_ref, scale_ref, shift_ref):
    taps = kernel_ref.shape[0]
    for c in range(kernel_ref.shape[1] // LANES):
        at = slice(c * LANES, (c + 1) * LANES)
        kernel_ref[:, at] = in_ref[c, 0:taps, :]
        scale_ref[:, at] = in_ref[c, taps : taps + 1, :]
        shift_ref[:, at] = in_ref[c, taps + 1 : taps + 2, :]


def on_device(frames, lengths, w_qkv, w_out, kernel, bn_scale, bn_shift, cotangent):
    blocks = lax.axis_size("seq")
    shares = lax.axis_size("dp")
    rows, width = frames.shape[1], frames.shape[2]
    hd = w_out.shape[1]
    total = rows * blocks
    taps = kernel.shape[0]
    small_rows = 16
    shape = jax.ShapeDtypeStruct
    x, g = frames[0], cotangent[0]

    with jax.named_scope("norm"):
        packed = pl.pallas_call(
            norm_kernel,
            in_specs=[VMEM, VMEM],
            out_specs=VMEM,
            out_shape=shape((rows + hd, width), BF16),
            compiler_params=params(16),
        )(x, w_out[0])
    with jax.named_scope("gather"):
        gathered = lax.all_gather(packed, "seq")
    with jax.named_scope("halo"):
        upward = [(i, i + 1) for i in range(blocks - 1)]
        downward = [(j, i) for i, j in upward]
        tails = jnp.concatenate([x[rows - EDGE :], g[rows - EDGE :]], axis=0)
        heads = jnp.concatenate([x[:EDGE], g[:EDGE]], axis=0)
        before = lax.ppermute(tails, "seq", upward)
        after = lax.ppermute(heads, "seq", downward)
    wt = w_qkv.reshape(width, 3 * hd).T

    with jax.named_scope("forward"):
        mixed, qkvt, k, v, soft = pl.pallas_call(
            forward_kernel,
            in_specs=[SMEM, ANYWHERE, VMEM],
            out_specs=[VMEM] * 5,
            out_shape=[
                shape((blocks, hd + 2 * EDGE, WIN), BF16),
                shape((3 * hd, total + 2 * WIN), BF16),
                shape((total + 2 * WIN, hd), BF16),
                shape((total + 2 * WIN, hd), BF16),
                shape((blocks, 3 * WIN, WIN), BF16),
            ],
            scratch_shapes=[
                pltpu.VMEM((blocks, WIN, width), BF16),
                pltpu.VMEM((blocks + 2, LANES, WIN), F32),
                pltpu.SemaphoreType.DMA((4,)),
            ],
            compiler_params=params(40),
        )(lengths, gathered, wt)
    with jax.named_scope("mixed_exchange"):
        mixed = lax.all_to_all(mixed, "seq", 0, 0)

    chunk = 256
    with jax.named_scope("middle"):
        place = jnp.stack([lax.axis_index("seq").astype(jnp.int32) * rows, lengths[0]])
        layer_out, d_mixed = pl.pallas_call(
            functools.partial(middle_kernel, chunk, total),
            in_specs=[SMEM, VMEM, ANYWHERE] + [VMEM] * 7,
            out_specs=[VMEM, VMEM],
            out_shape=[
                shape((rows, width), BF16),
                shape((blocks, hd + 2 * small_rows, rows), BF16),
            ],
            scratch_shapes=[
                pltpu.VMEM((blocks, hd, width), BF16),
                pltpu.VMEM((rows, width), BF16),
                pltpu.VMEM((rows + 2 * EDGE + taps - 1, chunk), F32),
                pltpu.VMEM((rows + 2 * EDGE, chunk), F32),
                pltpu.VMEM((small_rows, width), F32),
                pltpu.SemaphoreType.DMA,
            ],
            compiler_params=params(40),
        )(
            place, mixed, gathered, x, g, before, after, kernel,
            bn_scale.reshape(1, width), bn_shift.reshape(1, width),
        )
    with jax.named_scope("d_mixed_exchange"):
        d_mixed = lax.all_to_all(d_mixed, "seq", 0, 0)

    share = width // shares
    third = LANES // 8
    with jax.named_scope("backward"):
        messages = pl.pallas_call(
            functools.partial(backward_kernel, shares),
            in_specs=[VMEM, ANYWHERE] + [VMEM] * 4,
            out_specs=VMEM,
            out_shape=shape((shares, 2 * share + third + small_rows, LANES), BF16),
            scratch_shapes=[
                pltpu.VMEM((blocks, WIN, width), BF16),
                pltpu.VMEM((hd, total), BF16),
                pltpu.VMEM((hd, total + 2 * WIN), F32),
                pltpu.VMEM((hd, total + 2 * WIN), F32),
                pltpu.VMEM((3 * hd, total), BF16),
                pltpu.VMEM((width, 3 * LANES), F32),
                pltpu.SemaphoreType.DMA,
            ],
            compiler_params=params(40),
        )(d_mixed, gathered, qkvt, k, v, soft)
    with jax.named_scope("grad_exchange"):
        messages = lax.all_to_all(messages, "dp", 0, 0)
    with jax.named_scope("sum"):
        grad_qkv, small = pl.pallas_call(
            sum_kernel,
            in_specs=[VMEM],
            out_specs=[VMEM, VMEM],
            out_shape=[shape((share, 3 * hd), F32), shape((small_rows, LANES), F32)],
            compiler_params=params(16),
        )(messages)
    with jax.named_scope("small_gather"):
        small = lax.all_gather(small, "seq")
    with jax.named_scope("spread"):
        grad_kernel, grad_scale, grad_shift = pl.pallas_call(
            spread_kernel,
            in_specs=[VMEM],
            out_specs=[VMEM] * 3,
            out_shape=[shape((taps, width), F32), shape((1, width), F32), shape((1, width), F32)],
            compiler_params=params(16),
        )(small)
    return (
        layer_out[None],
        grad_qkv.reshape(share, 1, 3 * hd),
        grad_kernel,
        grad_scale.reshape(width),
        grad_shift.reshape(width),
    )


def solution(mesh):
    in_specs = (
        P("dp", "seq", None),
        P("dp"),
        P(None, "seq", None),
        P("seq", None, None),
        P(),
        P(),
        P(),
        P("dp", "seq", None),
    )
    out_specs = (P("dp", "seq", None), P("dp", "seq", None), P(), P(), P())
    return jax.shard_map(
        on_device, mesh=mesh, in_specs=in_specs, out_specs=out_specs, check_vma=False
    )
```

```python
import functools

import jax
import jax.numpy as jnp
from jax import lax
from jax.experimental import pallas as pl
from jax.experimental.pallas import tpu as pltpu
from jax.sharding import PartitionSpec as P

WIN = 128
EPS = 1e-05
FLOOR = 1.0
FAR = -1e30
EDGE = 8
LANES = 128
F32 = jnp.float32
BF16 = jnp.bfloat16

VMEM = pl.BlockSpec(memory_space=pltpu.VMEM)
SMEM = pl.BlockSpec(memory_space=pltpu.SMEM)
HBM = pl.BlockSpec(memory_space=pltpu.HBM)


def params(mib):
    return pltpu.CompilerParams(vmem_limit_bytes=mib * 1024 * 1024)


def dot(a, b, dims):
    return lax.dot_general(a, b, ((dims[:1], dims[1:]), ((), ())), preferred_element_type=F32)


def norm_kernel(x_ref, normed_ref):
    values = x_ref[...].astype(F32)
    center = values - jnp.mean(values, axis=-1, keepdims=True)
    spread = jnp.mean(center * center, axis=-1, keepdims=True)
    normed_ref[...] = (center * lax.rsqrt(spread + EPS)).astype(BF16)


def forward_kernel(
    len_ref, gathered_ref, wt_ref, out_ref, qkvt_out, v_out, soft_out,
    normed, mixed, qkvt_ref, k_ref, v_ref, soft_ref, bias, sems, out_sems
):
    blocks = gathered_ref.shape[0]
    hd = v_ref.shape[1]
    total = blocks * WIN
    per = blocks // sems.shape[0]
    kept = [
        pltpu.make_async_copy(qkvt_ref, qkvt_out, out_sems.at[0]),
        pltpu.make_async_copy(v_ref, v_out, out_sems.at[1]),
    ] + [
        pltpu.make_async_copy(
            soft_ref.at[pl.ds(c * per, per)], soft_out.at[pl.ds(c * per, per)], out_sems.at[2 + c]
        )
        for c in range(sems.shape[0])
    ]
    copies = [
        pltpu.make_async_copy(
            gathered_ref.at[pl.ds(c * per, per)],
            normed.at[pl.ds(c * per, per)],
            sems.at[c],
        )
        for c in range(sems.shape[0])
    ]
    for copy in copies:
        copy.start()
    length = len_ref[0]
    key = lax.broadcasted_iota(jnp.int32, (3 * WIN, WIN), 0)
    query = lax.broadcasted_iota(jnp.int32, (3 * WIN, WIN), 1)
    near = (key >= query) & (key - query <= 2 * WIN)
    bias[...] = jnp.where(near, 0.0, FAR)
    extra = k_ref.shape[1] - hd
    position = lax.broadcasted_iota(jnp.int32, (total + 2 * WIN, extra), 0) - WIN
    dead = (position < 0) | (position >= length)
    k_ref[:, hd:] = jnp.where(dead, FAR, 0.0).astype(BF16)
    ones = (lax.broadcasted_iota(jnp.int32, (extra, WIN), 0) == 0).astype(F32).astype(BF16)
    for edge in (slice(0, WIN), slice(WIN + total, 2 * WIN + total)):
        qkvt_ref[:, edge] = jnp.zeros((3 * hd, WIN), BF16)
        k_ref[edge, 0:hd] = jnp.zeros((WIN, hd), BF16)
        v_ref[edge, :] = jnp.zeros((WIN, hd), BF16)
    mixed[0] = jnp.zeros(mixed.shape[1:], F32)
    mixed[blocks + 1] = jnp.zeros(mixed.shape[1:], F32)
    wt = wt_ref[...]
    for c, copy in enumerate(copies):
        copy.wait()
        rows = normed[c * per : (c + 1) * per].reshape(per * WIN, normed.shape[2])
        part = dot(wt, rows, (1, 1))
        at = slice(WIN + c * per * WIN, WIN + (c + 1) * per * WIN)
        qkvt_ref[:, at] = part.astype(BF16)
        k_ref[at, 0:hd] = part[hd : 2 * hd].T.astype(BF16)
        v_ref[at, :] = part[2 * hd :].T.astype(BF16)

    for copy in kept[:2]:
        copy.start()
    column = lax.broadcasted_iota(jnp.int32, (1, WIN), 1)
    scale = hd ** (-0.5)

    def attend(i, carry):
        start = pl.multiple_of(i * WIN, WIN)
        q = qkvt_ref[0:hd, pl.ds(pl.multiple_of(start + WIN, WIN), WIN)]
        q = jnp.concatenate([q, ones], axis=0)
        scores = dot(k_ref[pl.ds(start, 3 * WIN), :], q, (1, 0)) * scale + bias[...]
        top = jnp.max(scores, axis=0, keepdims=True)
        expo = jnp.exp(scores - top)
        denominator = jnp.maximum(jnp.sum(expo, axis=0, keepdims=True), FLOOR)
        soft = (expo * (1.0 / denominator)).astype(BF16)
        soft_ref[i] = soft
        result = dot(qkvt_ref[2 * hd : 3 * hd, pl.ds(start, 3 * WIN)], soft, (1, 0))
        result = jnp.where(column + start < length, result, 0.0)
        mixed[i + 1, 0:hd, :] = result
        mixed[i + 1, hd:, :] = jnp.zeros((mixed.shape[1] - hd, WIN), F32)
        out_ref[i, 0:hd, :] = result.astype(BF16)
        return carry

    for c in range(sems.shape[0]):
        lax.fori_loop(c * per, (c + 1) * per, attend, 0, unroll=True)
        kept[2 + c].start()

    def edges(i, carry):
        both = jnp.where(column < EDGE, mixed[i + 2], mixed[i]).T
        rows = jnp.concatenate([both[WIN - EDGE :], both[:EDGE]], axis=0)
        out_ref[i, hd:, :] = rows.astype(BF16)
        return carry

    lax.fori_loop(0, blocks, edges, 0, unroll=4)
    for copy in kept:
        copy.wait()


def middle_kernel(
    total, place_ref, mix_in, x_in, g_in, prev_in, next_in, own_ref, near_ref, twin_ref, far_ref,
    twin_far_ref, taps_ref, scale_ref, shift_ref, layer_out, out_ref, mix_ref, x_ref, g_ref,
    prev_ref, next_ref, layer_ref, weight, d_hidden, masked, d_conv, small, sems, more_sems
):
    inputs = [
        pltpu.make_async_copy(source, target, more_sems.at[i])
        for i, (source, target) in enumerate((
            (mix_in, mix_ref), (prev_in, prev_ref), (next_in, next_ref), (x_in, x_ref),
            (g_in, g_ref),
        ))
    ]
    for copy in inputs:
        copy.start()
    heads, width = mix_ref.shape[0], x_ref.shape[1]
    rows = x_ref.shape[0]
    quarters, _, hd, chunk = weight.shape
    core = lax.rem(place_ref[0], 2)
    half = heads // 2
    first, last = pl.ds(0, half), pl.ds(half, half)
    pieces = (
        (0, own_ref.at[first], own_ref.at[last]),
        (2 * core - 1, near_ref.at[first], near_ref.at[last]),
        (1 - 2 * core, twin_ref.at[last], twin_ref.at[first]),
        (2, far_ref, twin_far_ref),
    )

    def fetch(quarter, lower, upper):
        for j, piece in enumerate((lower, upper)):
            target = weight.at[quarter, pl.ds(j * half, half)]
            pltpu.make_async_copy(piece, target, sems.at[quarter, j]).start()

    for quarter in range(quarters):
        for step, lower, upper in pieces:
            holds = lax.rem(place_ref[2] + step + quarters, quarters) == quarter
            pl.when(holds)(functools.partial(fetch, quarter, lower, upper))
    taps_count = taps_ref.shape[0]
    reach = (taps_count - 1) // 2
    ext = rows + 2 * EDGE
    length = place_ref[1]
    base = place_ref[0] * rows
    order = [core + 2 * j for j in range(heads // 2)] + [1 - core + 2 * j for j in range(heads // 2)]
    inputs[0].wait()
    body = jnp.concatenate([mix_ref[h, 0:hd, :] for h in order], axis=0).T
    fringe = jnp.concatenate([mix_ref[h, hd:, 0:hd] for h in order], axis=1)
    mix = jnp.concatenate([body, fringe], axis=0)
    pos = lax.broadcasted_iota(jnp.int32, (ext, 1), 0) + (base - EDGE)
    live = (pos >= 0) & (pos < length)
    inside = (pos >= 0) & (pos < total)
    live_here = live[EDGE : EDGE + rows]
    small[...] = jnp.zeros(small.shape, F32)
    masked[0:reach, :] = jnp.zeros((reach, chunk), F32)
    masked[reach + ext :, :] = jnp.zeros((reach, chunk), F32)
    for copy in inputs[1:]:
        copy.wait()
    for c in range(quarters):
        at = slice(c * chunk, (c + 1) * chunk)
        for j in range(2):
            target = weight.at[c, pl.ds(j * half, half)]
            pltpu.make_async_copy(target, target, sems.at[c, j]).wait()
        w = weight[c].reshape(heads * hd, chunk)
        attended = dot(mix, w, (1, 0))
        attended = jnp.concatenate(
            [attended[rows : rows + EDGE], attended[:rows], attended[rows + EDGE :]], axis=0
        )
        before = prev_ref[:, at].astype(F32)
        after = next_ref[:, at].astype(F32)
        frames = jnp.concatenate([before[:EDGE], x_ref[:, at].astype(F32), after[:EDGE]], axis=0)
        upstream = jnp.concatenate([before[EDGE:], g_ref[:, at].astype(F32), after[EDGE:]], axis=0)
        hidden = (frames + attended).astype(BF16).astype(F32)
        masked[reach : reach + ext, :] = jnp.where(live, hidden, 0.0)
        taps = taps_ref[:, at].astype(F32)
        conv = jnp.zeros((ext, chunk), F32)
        for k in range(taps_count):
            conv = conv + masked[k : k + ext, :] * taps[k : k + 1]
        gain = scale_ref[:, at]
        shifted = conv * gain + shift_ref[:, at]
        sigmoid = jax.nn.sigmoid(shifted)
        d_shifted = upstream * sigmoid * (1.0 + shifted * (1.0 - sigmoid))
        own = slice(EDGE, EDGE + rows)
        layer_ref[:, at] = (hidden[own] + (shifted * sigmoid)[own]).astype(BF16)
        d_own = d_shifted[own]
        small[taps_count : taps_count + 1, at] = jnp.sum(d_own * conv[own], axis=0, keepdims=True)
        small[taps_count + 1 : taps_count + 2, at] = jnp.sum(d_own, axis=0, keepdims=True)
        d_conv[...] = jnp.where(inside, d_shifted * gain, 0.0)
        d_conv_own = d_own * gain
        spread = jnp.zeros((rows, chunk), F32)
        for k in range(taps_count):
            small[k : k + 1, at] = jnp.sum(
                d_conv_own * masked[EDGE + k : EDGE + k + rows, :], axis=0, keepdims=True
            )
            first = EDGE + reach - k
            spread = spread + taps[k : k + 1] * d_conv[first : first + rows, :]
        d_hidden[:, at] = (upstream[own] + jnp.where(live_here, spread, 0.0)).astype(BF16)
    result = pltpu.make_async_copy(layer_ref, layer_out, more_sems.at[len(inputs)])
    result.start()
    column = lax.broadcasted_iota(jnp.int32, (1, rows), 1) + base
    group = 4
    for h in range(0, heads, group):
        d_mixed = jnp.zeros((group * hd, rows), F32)
        for c in range(quarters):
            w = weight[c, h : h + group].reshape(group * hd, chunk)
            d_mixed = d_mixed + dot(w, d_hidden[:, c * chunk : (c + 1) * chunk], (1, 1))
        d_mixed = jnp.where(column < length, d_mixed, 0.0).astype(BF16)
        for j in range(group):
            out_ref[order[h + j], 0:hd, :] = d_mixed[j * hd : (j + 1) * hd]
    high = small[...].astype(BF16)
    low = (small[...] - high.astype(F32)).astype(BF16)
    more = small.shape[0]
    for h in range(heads):
        if (h + 1) * LANES <= width:
            at = slice(h * LANES, (h + 1) * LANES)
            out_ref[h, hd : hd + more, :] = high[:, at]
            out_ref[h, hd + more :, :] = low[:, at]
        else:
            out_ref[h, hd:, :] = jnp.zeros((2 * more, rows), BF16)
    result.wait()


def backward_kernel(
    shares, in_ref, gathered_ref, qkvt_in, v_in, soft_in, out_ref,
    normed, d_query, d_key, d_value, joined, grad, qkvt_ref, v_ref, soft_ref, sems
):
    blocks, width = gathered_ref.shape[0], gathered_ref.shape[2]
    hd = v_ref.shape[1]
    total = blocks * WIN
    groups = sems.shape[0] - 3
    per = blocks // groups
    copies = [
        pltpu.make_async_copy(v_in, v_ref, sems.at[0]),
        pltpu.make_async_copy(qkvt_in, qkvt_ref, sems.at[1]),
    ] + [
        pltpu.make_async_copy(
            soft_in.at[pl.ds(c * per, per)], soft_ref.at[pl.ds(c * per, per)], sems.at[2 + c]
        )
        for c in range(groups)
    ]
    for copy in copies:
        copy.start()
    fetch = pltpu.make_async_copy(gathered_ref, normed, sems.at[2 + groups])
    d_key[...] = jnp.zeros(d_key.shape, F32)
    d_value[...] = jnp.zeros(d_value.shape, F32)
    scale = hd ** (-0.5)

    def attend(i, carry):
        start = pl.multiple_of(i * WIN, WIN)
        own = pl.ds(pl.multiple_of(start + WIN, WIN), WIN)
        window = pl.ds(start, 3 * WIN)
        d_mixed = in_ref[i, 0:hd, :]
        soft = soft_ref[i]
        wide = soft.astype(F32)
        d_soft = dot(v_ref[window, :], d_mixed, (1, 0))
        inner = jnp.sum(wide * d_soft, axis=0, keepdims=True)
        d_scores = (wide * (d_soft - inner) * scale).astype(BF16)
        d_query[:, pl.ds(start, WIN)] = dot(qkvt_ref[hd : 2 * hd, window], d_scores, (1, 0)).astype(BF16)
        d_key[:, window] += dot(qkvt_ref[0:hd, own], d_scores, (1, 1))
        d_value[:, window] += dot(d_mixed, soft, (1, 1))
        return carry

    copies[0].wait()
    copies[1].wait()
    fetch.start()
    for c in range(groups):
        copies[2 + c].wait()
        lax.fori_loop(c * per, (c + 1) * per, attend, 0, unroll=True)
    joined[0:hd, :] = d_query[...]
    joined[hd : 2 * hd, :] = d_key[:, WIN : WIN + total].astype(BF16)
    joined[2 * hd :, :] = d_value[:, WIN : WIN + total].astype(BF16)
    fetch.wait()
    rest = 3 * hd - 2 * LANES
    repeats = LANES // rest
    step = 512
    for c in range(width // step):
        at = slice(c * step, (c + 1) * step)
        rows = normed[:, :, at].reshape(total, step)
        part = dot(joined[...], rows, (1, 0))
        tail = part[2 * LANES :]
        grad[at, :] = jnp.concatenate([part[: 2 * LANES]] + [tail] * repeats, axis=0).T
    share = width // shares
    third = share // (repeats - 1)
    lane = lax.broadcasted_iota(jnp.int32, (1, LANES), 1) // rest
    for d in range(shares):
        at = slice(d * share, (d + 1) * share)
        out_ref[d, 0:share, :] = grad[at, 0:LANES].astype(BF16)
        out_ref[d, share : 2 * share, :] = grad[at, LANES : 2 * LANES].astype(BF16)
        packed = jnp.zeros((third, LANES), F32)
        for j in range(repeats - 1):
            first = d * share + j * third
            packed = jnp.where(lane == j, grad[first : first + third, 2 * LANES :], packed)
        out_ref[d, 2 * share :, :] = packed.astype(BF16)


def sum_kernel(in_ref, grad_ref):
    share, columns = grad_ref.shape[0], grad_ref.shape[2]
    third = in_ref.shape[1] - 2 * share
    rest = columns - 2 * LANES
    summed = jnp.sum(in_ref[...].astype(F32), axis=0)
    grad_ref[:, 0, 0:LANES] = summed[0:share]
    grad_ref[:, 0, LANES : 2 * LANES] = summed[share : 2 * share]
    for j in range(share // third):
        grad_ref[j * third : (j + 1) * third, 0, 2 * LANES :] = summed[
            2 * share : 2 * share + third, j * rest : (j + 1) * rest
        ]


def spread_kernel(in_ref, kernel_ref, scale_ref, shift_ref):
    taps = kernel_ref.shape[0]
    for c in range(kernel_ref.shape[1] // LANES):
        at = slice(c * LANES, (c + 1) * LANES)
        kernel_ref[:, at] = in_ref[c, 0:taps, :]
        scale_ref[at] = in_ref[c, taps, :]
        shift_ref[at] = in_ref[c, taps + 1, :]


def on_device(frames, lengths, w_qkv, w_out, kernel, bn_scale, bn_shift, cotangent):
    blocks = lax.axis_size("seq")
    shares = lax.axis_size("dp")
    rows, width = frames.shape[1], frames.shape[2]
    hd = w_out.shape[1]
    total = rows * blocks
    taps = kernel.shape[0]
    small_rows = 16
    shape = jax.ShapeDtypeStruct
    x, g = frames[0], cotangent[0]

    with jax.named_scope("norm"):
        normed = pl.pallas_call(
            norm_kernel,
            in_specs=[VMEM],
            out_specs=VMEM,
            out_shape=shape((rows, width), BF16),
            compiler_params=params(16),
        )(x)
    with jax.named_scope("gather"):
        gathered = lax.all_gather(normed, "seq")
    with jax.named_scope("halo"):
        upward = [(i, i + 1) for i in range(blocks - 1)]
        downward = [(j, i) for i, j in upward]
        tails = jnp.concatenate([x[rows - EDGE :], g[rows - EDGE :]], axis=0)
        heads = jnp.concatenate([x[:EDGE], g[:EDGE]], axis=0)
        before = lax.ppermute(tails, "seq", upward)
        after = lax.ppermute(heads, "seq", downward)
    firsts = 4
    per = shares // firsts
    chunk = width // firsts
    with jax.named_scope("w_out_columns"):
        quarter = lax.dynamic_slice_in_dim(
            w_out, lax.axis_index("dp") // per * chunk, chunk, axis=2
        )
        same = [list(range(c, blocks, 2)) for c in range(2)]
        twins = [(i, i ^ 1) for i in range(blocks)]
        columns = jnp.broadcast_to(quarter, (blocks // 2, hd, chunk))
        columns = lax.all_to_all(columns, "seq", 0, 0, axis_index_groups=same)
        columns = jnp.concatenate([columns, lax.ppermute(columns, "seq", twins)], axis=0)
        def onward(dp, seq):
            first = (dp // per + 1 - 2 * (seq % 2)) % firsts
            return (first * per + dp % per) * blocks + seq

        ring = [(d * blocks + i, onward(d, i)) for d in range(shares) for i in range(blocks)]
        near = lax.ppermute(columns, ("dp", "seq"), ring)
        near, before, after = lax.optimization_barrier((near, before, after))
        twin = lax.ppermute(near, "seq", twins)
        far = lax.ppermute(near[: blocks // 2], ("dp", "seq"), ring)
        twin_far = lax.ppermute(far, "seq", twins)
    gathered, near = lax.optimization_barrier((gathered, near))
    wt = w_qkv.reshape(width, 3 * hd).T

    with jax.named_scope("forward"):
        mixed, qkvt, v, soft = pl.pallas_call(
            forward_kernel,
            in_specs=[SMEM, HBM, VMEM],
            out_specs=[VMEM] + [HBM] * 3,
            out_shape=[
                shape((blocks, hd + 2 * EDGE, WIN), BF16),
                shape((3 * hd, total + 2 * WIN), BF16),
                shape((total + 2 * WIN, hd), BF16),
                shape((blocks, 3 * WIN, WIN), BF16),
            ],
            scratch_shapes=[
                pltpu.VMEM((blocks, WIN, width), BF16),
                pltpu.VMEM((blocks + 2, LANES, WIN), F32),
                pltpu.VMEM((3 * hd, total + 2 * WIN), BF16),
                pltpu.VMEM((total + 2 * WIN, LANES), BF16),
                pltpu.VMEM((total + 2 * WIN, hd), BF16),
                pltpu.VMEM((blocks, 3 * WIN, WIN), BF16),
                pltpu.VMEM((3 * WIN, WIN), F32),
                pltpu.SemaphoreType.DMA((4,)),
                pltpu.SemaphoreType.DMA((6,)),
            ],
            compiler_params=params(58),
        )(lengths, gathered, wt)
    with jax.named_scope("mixed_exchange"):
        mixed = lax.all_to_all(mixed, "seq", 0, 0)

    with jax.named_scope("middle"):
        place = jnp.stack([lax.axis_index("seq"), lengths[0], lax.axis_index("dp") // per])
        layer_out, d_mixed = pl.pallas_call(
            functools.partial(middle_kernel, total),
            in_specs=[SMEM] + [HBM] * 10 + [VMEM] * 3,
            out_specs=[HBM, VMEM],
            out_shape=[
                shape((rows, width), BF16),
                shape((blocks, hd + 2 * small_rows, rows), BF16),
            ],
            scratch_shapes=[
                pltpu.VMEM(mixed.shape, BF16),
                pltpu.VMEM((rows, width), BF16),
                pltpu.VMEM((rows, width), BF16),
                pltpu.VMEM((2 * EDGE, width), BF16),
                pltpu.VMEM((2 * EDGE, width), BF16),
                pltpu.VMEM((rows, width), BF16),
                pltpu.VMEM((firsts, blocks, hd, chunk), BF16),
                pltpu.VMEM((rows, width), BF16),
                pltpu.VMEM((rows + 2 * EDGE + taps - 1, chunk), F32),
                pltpu.VMEM((rows + 2 * EDGE, chunk), F32),
                pltpu.VMEM((small_rows, width), F32),
                pltpu.SemaphoreType.DMA((firsts, 2)),
                pltpu.SemaphoreType.DMA((6,)),
            ],
            compiler_params=params(60),
        )(
            place, mixed, x, g, before, after, columns, near, twin, far, twin_far, kernel,
            bn_scale.reshape(1, width), bn_shift.reshape(1, width),
        )
    with jax.named_scope("d_mixed_exchange"):
        d_mixed = lax.all_to_all(d_mixed, "seq", 0, 0)

    share = width // shares
    third = LANES // 8
    across = [[i * per + j for i in range(firsts)] for j in range(per)]
    along = [[i * per + j for j in range(per)] for i in range(firsts)]
    with jax.named_scope("small_sums"):
        small = jnp.sum(d_mixed[:, hd:].astype(F32).reshape(2 * blocks, small_rows, LANES), axis=0)
        small = lax.all_to_all(
            jnp.broadcast_to(small, (per,) + small.shape), "dp", 0, 0, axis_index_groups=along
        )
    with jax.named_scope("backward"):
        messages = pl.pallas_call(
            functools.partial(backward_kernel, shares),
            in_specs=[VMEM] + [HBM] * 4,
            out_specs=VMEM,
            out_shape=shape((shares, 2 * share + third, LANES), BF16),
            scratch_shapes=[
                pltpu.VMEM((blocks, WIN, width), BF16),
                pltpu.VMEM((hd, total), BF16),
                pltpu.VMEM((hd, total + 2 * WIN), F32),
                pltpu.VMEM((hd, total + 2 * WIN), F32),
                pltpu.VMEM((3 * hd, total), BF16),
                pltpu.VMEM((width, 3 * LANES), F32),
                pltpu.VMEM((3 * hd, total + 2 * WIN), BF16),
                pltpu.VMEM((total + 2 * WIN, hd), BF16),
                pltpu.VMEM((blocks, 3 * WIN, WIN), BF16),
                pltpu.SemaphoreType.DMA((7,)),
            ],
            compiler_params=params(56),
        )(d_mixed, gathered, qkvt, v, soft)
    messages, small = lax.optimization_barrier((messages, small))
    with jax.named_scope("grad_exchange"):
        messages = lax.all_to_all(messages, "dp", 0, 0)
    with jax.named_scope("small_gathers"):
        small = jnp.sum(small, axis=0)
        small = jnp.sum(lax.all_gather(small, "dp", axis_index_groups=across), axis=0)
        small = lax.all_gather(small, "seq")
    with jax.named_scope("sum"):
        grad_qkv = pl.pallas_call(
            sum_kernel,
            in_specs=[VMEM],
            out_specs=VMEM,
            out_shape=shape((share, 1, 3 * hd), F32),
            compiler_params=params(16),
        )(messages)
    with jax.named_scope("spread"):
        grad_kernel, grad_scale, grad_shift = pl.pallas_call(
            spread_kernel,
            in_specs=[VMEM],
            out_specs=[VMEM] * 3,
            out_shape=[shape((taps, width), F32), shape((width,), F32), shape((width,), F32)],
            compiler_params=params(16),
        )(small)
    return (
        layer_out[None],
        grad_qkv,
        grad_kernel,
        grad_scale,
        grad_shift,
    )


def solution(mesh):
    in_specs = (
        P("dp", "seq", None),
        P("dp"),
        P(None, "seq", None),
        P("seq", None, None),
        P(),
        P(),
        P(),
        P("dp", "seq", None),
    )
    out_specs = (P("dp", "seq", None), P("dp", "seq", None), P(), P(), P())
    return jax.shard_map(
        on_device, mesh=mesh, in_specs=in_specs, out_specs=out_specs, check_vma=False
    )
```

```python
import functools

import jax
import jax.numpy as jnp
from jax import lax
from jax.experimental import pallas as pl
from jax.experimental.pallas import tpu as pltpu
from jax.sharding import PartitionSpec as P

WIN = 128
EPS = 1e-05
FLOOR = 1.0
FAR = -1e30
EDGE = 8
LANES = 128
F32 = jnp.float32
BF16 = jnp.bfloat16

VMEM = pl.BlockSpec(memory_space=pltpu.VMEM)
SMEM = pl.BlockSpec(memory_space=pltpu.SMEM)
HBM = pl.BlockSpec(memory_space=pltpu.HBM)


def params(mib):
    return pltpu.CompilerParams(vmem_limit_bytes=mib * 1024 * 1024)


def dot(a, b, dims):
    return lax.dot_general(a, b, ((dims[:1], dims[1:]), ((), ())), preferred_element_type=F32)


def norm_kernel(x_in, normed_out, x_ref, normed_ref, sems):
    parts = sems.shape[1]
    step = x_ref.shape[0] // parts
    places = [pl.ds(c * step, step) for c in range(parts)]
    takes = [
        pltpu.make_async_copy(x_in.at[at], x_ref.at[at], sems.at[0, c])
        for c, at in enumerate(places)
    ]
    gives = [
        pltpu.make_async_copy(normed_ref.at[at], normed_out.at[at], sems.at[1, c])
        for c, at in enumerate(places)
    ]
    for take in takes:
        take.start()
    for at, take, give in zip(places, takes, gives):
        take.wait()
        values = x_ref[at, :].astype(F32)
        center = values - jnp.mean(values, axis=-1, keepdims=True)
        spread = jnp.mean(center * center, axis=-1, keepdims=True)
        normed_ref[at, :] = (center * lax.rsqrt(spread + EPS)).astype(BF16)
        give.start()
    for give in gives:
        give.wait()


def forward_kernel(
    len_ref, gathered_ref, wt_ref, out_ref, qkvt_out, v_out, soft_out,
    normed, mixed, qkvt_ref, k_ref, v_ref, soft_ref, bias, sems, out_sems
):
    blocks = gathered_ref.shape[0]
    hd = v_ref.shape[1]
    total = blocks * WIN
    per = blocks // sems.shape[0]
    sends = []

    def send(source, target):
        sends.append(pltpu.make_async_copy(source, target, out_sems.at[len(sends)]))
        sends[-1].start()

    copies = [
        pltpu.make_async_copy(
            gathered_ref.at[pl.ds(c * per, per)],
            normed.at[pl.ds(c * per, per)],
            sems.at[c],
        )
        for c in range(sems.shape[0])
    ]
    for copy in copies:
        copy.start()
    length = len_ref[0]
    key = lax.broadcasted_iota(jnp.int32, (3 * WIN, WIN), 0)
    query = lax.broadcasted_iota(jnp.int32, (3 * WIN, WIN), 1)
    near = (key >= query) & (key - query <= 2 * WIN)
    bias[...] = jnp.where(near, 0.0, FAR)
    extra = k_ref.shape[1] - hd
    position = lax.broadcasted_iota(jnp.int32, (total + 2 * WIN, extra), 0) - WIN
    dead = (position < 0) | (position >= length)
    k_ref[:, hd:] = jnp.where(dead, FAR, 0.0).astype(BF16)
    ones = (lax.broadcasted_iota(jnp.int32, (extra, WIN), 0) == 0).astype(F32).astype(BF16)
    for edge in (slice(0, WIN), slice(WIN + total, 2 * WIN + total)):
        qkvt_ref[:, edge] = jnp.zeros((3 * hd, WIN), BF16)
        k_ref[edge, 0:hd] = jnp.zeros((WIN, hd), BF16)
        v_ref[edge, :] = jnp.zeros((WIN, hd), BF16)
    mixed[0] = jnp.zeros(mixed.shape[1:], F32)
    mixed[blocks + 1] = jnp.zeros(mixed.shape[1:], F32)
    column = lax.broadcasted_iota(jnp.int32, (1, WIN), 1)
    scale = hd ** (-0.5)

    def attend(i, carry):
        start = pl.multiple_of(i * WIN, WIN)
        q = qkvt_ref[0:hd, pl.ds(pl.multiple_of(start + WIN, WIN), WIN)]
        q = jnp.concatenate([q, ones], axis=0)
        scores = dot(k_ref[pl.ds(start, 3 * WIN), :], q, (1, 0)) * scale + bias[...]
        top = jnp.max(scores, axis=0, keepdims=True)
        expo = jnp.exp(scores - top)
        denominator = jnp.maximum(jnp.sum(expo, axis=0, keepdims=True), FLOOR)
        soft = (expo * (1.0 / denominator)).astype(BF16)
        soft_ref[i] = soft
        result = dot(qkvt_ref[2 * hd : 3 * hd, pl.ds(start, 3 * WIN)], soft, (1, 0))
        result = jnp.where(column + start < length, result, 0.0)
        mixed[i + 1, 0:hd, :] = result
        mixed[i + 1, hd:, :] = jnp.zeros((mixed.shape[1] - hd, WIN), F32)
        out_ref[i, 0:hd, :] = result.astype(BF16)
        return carry

    wt = wt_ref[...]
    for c, copy in enumerate(copies):
        copy.wait()
        rows = normed[c * per : (c + 1) * per].reshape(per * WIN, normed.shape[2])
        part = dot(wt, rows, (1, 1))
        at = slice(WIN + c * per * WIN, WIN + (c + 1) * per * WIN)
        qkvt_ref[:, at] = part.astype(BF16)
        k_ref[at, 0:hd] = part[hd : 2 * hd].T.astype(BF16)
        v_ref[at, :] = part[2 * hd :].T.astype(BF16)
        final = c == len(copies) - 1
        low, high = at.start - WIN * (c == 0), at.stop + WIN * final
        done = pl.ds(low, high - low)
        send(qkvt_ref.at[:, done], qkvt_out.at[:, done])
        send(v_ref.at[done], v_out.at[done])
        first, stop = max(c * per - 1, 0), (c + 1) * per - 1 + final
        lax.fori_loop(first, stop, attend, 0, unroll=True)
        done = pl.ds(first, stop - first)
        send(soft_ref.at[done], soft_out.at[done])

    def edges(i, carry):
        both = jnp.where(column < EDGE, mixed[i + 2], mixed[i]).T
        rows = jnp.concatenate([both[WIN - EDGE :], both[:EDGE]], axis=0)
        out_ref[i, hd:, :] = rows.astype(BF16)
        return carry

    lax.fori_loop(0, blocks, edges, 0, unroll=4)
    for copy in sends:
        copy.wait()


def middle_kernel(
    total, place_ref, mix_in, x_in, g_in, prev_in, next_in, own_ref, near_ref, twin_ref, far_ref,
    taps_ref, scale_ref, shift_ref, layer_out, out_ref, mix_ref, x_ref, g_ref,
    prev_ref, next_ref, layer_ref, weight, d_hidden, masked, d_conv, small, sems, more_sems
):
    inputs = [
        pltpu.make_async_copy(source, target, more_sems.at[i])
        for i, (source, target) in enumerate((
            (mix_in, mix_ref), (prev_in, prev_ref), (next_in, next_ref), (x_in, x_ref),
            (g_in, g_ref),
        ))
    ]
    for copy in inputs:
        copy.start()
    heads, width = mix_ref.shape[0], x_ref.shape[1]
    rows = x_ref.shape[0]
    quarters, _, hd, chunk = weight.shape
    core = lax.rem(place_ref[0], 2)
    half = heads // 2
    first, last = pl.ds(0, half), pl.ds(half, half)
    pieces = (
        (0, own_ref.at[first], own_ref.at[last]),
        (2 * core - 1, near_ref.at[first], near_ref.at[last]),
        (1 - 2 * core, twin_ref.at[last], twin_ref.at[first]),
        (2, far_ref.at[first], far_ref.at[last]),
    )

    def fetch(quarter, lower, upper):
        for j, piece in enumerate((lower, upper)):
            target = weight.at[quarter, pl.ds(j * half, half)]
            pltpu.make_async_copy(piece, target, sems.at[quarter, j]).start()

    for quarter in range(quarters):
        for step, lower, upper in pieces:
            holds = lax.rem(place_ref[2] + step + quarters, quarters) == quarter
            pl.when(holds)(functools.partial(fetch, quarter, lower, upper))
    taps_count = taps_ref.shape[0]
    reach = (taps_count - 1) // 2
    ext = rows + 2 * EDGE
    length = place_ref[1]
    base = place_ref[0] * rows
    order = [core + 2 * j for j in range(heads // 2)] + [1 - core + 2 * j for j in range(heads // 2)]
    inputs[0].wait()
    body = jnp.concatenate([mix_ref[h, 0:hd, :] for h in order], axis=0).T
    fringe = jnp.concatenate([mix_ref[h, hd:, 0:hd] for h in order], axis=1)
    mix = jnp.concatenate([body, fringe], axis=0)
    pos = lax.broadcasted_iota(jnp.int32, (ext, 1), 0) + (base - EDGE)
    live = (pos >= 0) & (pos < length)
    inside = (pos >= 0) & (pos < total)
    live_here = live[EDGE : EDGE + rows]
    small[...] = jnp.zeros(small.shape, F32)
    masked[0:reach, :] = jnp.zeros((reach, chunk), F32)
    masked[reach + ext :, :] = jnp.zeros((reach, chunk), F32)
    for copy in inputs[1:]:
        copy.wait()
    for c in range(quarters):
        at = slice(c * chunk, (c + 1) * chunk)
        for j in range(2):
            target = weight.at[c, pl.ds(j * half, half)]
            pltpu.make_async_copy(target, target, sems.at[c, j]).wait()
        w = weight[c].reshape(heads * hd, chunk)
        attended = dot(mix, w, (1, 0))
        attended = jnp.concatenate(
            [attended[rows : rows + EDGE], attended[:rows], attended[rows + EDGE :]], axis=0
        )
        before = prev_ref[:, at].astype(F32)
        after = next_ref[:, at].astype(F32)
        frames = jnp.concatenate([before[:EDGE], x_ref[:, at].astype(F32), after[:EDGE]], axis=0)
        upstream = jnp.concatenate([before[EDGE:], g_ref[:, at].astype(F32), after[EDGE:]], axis=0)
        hidden = (frames + attended).astype(BF16).astype(F32)
        masked[reach : reach + ext, :] = jnp.where(live, hidden, 0.0)
        taps = taps_ref[:, at].astype(F32)
        conv = jnp.zeros((ext, chunk), F32)
        for k in range(taps_count):
            conv = conv + masked[k : k + ext, :] * taps[k : k + 1]
        gain = scale_ref[:, at]
        shifted = conv * gain + shift_ref[:, at]
        sigmoid = jax.nn.sigmoid(shifted)
        d_shifted = upstream * sigmoid * (1.0 + shifted * (1.0 - sigmoid))
        own = slice(EDGE, EDGE + rows)
        layer_ref[:, at] = (hidden[own] + (shifted * sigmoid)[own]).astype(BF16)
        d_own = d_shifted[own]
        small[taps_count : taps_count + 1, at] = jnp.sum(d_own * conv[own], axis=0, keepdims=True)
        small[taps_count + 1 : taps_count + 2, at] = jnp.sum(d_own, axis=0, keepdims=True)
        d_conv[...] = jnp.where(inside, d_shifted * gain, 0.0)
        d_conv_own = d_own * gain
        spread = jnp.zeros((rows, chunk), F32)
        for k in range(taps_count):
            small[k : k + 1, at] = jnp.sum(
                d_conv_own * masked[EDGE + k : EDGE + k + rows, :], axis=0, keepdims=True
            )
            first = EDGE + reach - k
            spread = spread + taps[k : k + 1] * d_conv[first : first + rows, :]
        d_hidden[:, at] = (upstream[own] + jnp.where(live_here, spread, 0.0)).astype(BF16)
    result = pltpu.make_async_copy(layer_ref, layer_out, more_sems.at[len(inputs)])
    result.start()
    column = lax.broadcasted_iota(jnp.int32, (1, rows), 1) + base
    group = 4
    for h in range(0, heads, group):
        d_mixed = jnp.zeros((group * hd, rows), F32)
        for c in range(quarters):
            w = weight[c, h : h + group].reshape(group * hd, chunk)
            d_mixed = d_mixed + dot(w, d_hidden[:, c * chunk : (c + 1) * chunk], (1, 1))
        d_mixed = jnp.where(column < length, d_mixed, 0.0).astype(BF16)
        for j in range(group):
            out_ref[order[h + j], 0:hd, :] = d_mixed[j * hd : (j + 1) * hd]
    sums = small[...].astype(BF16)
    for h in range(heads):
        if (h + 1) * LANES <= width:
            out_ref[h, hd:, :] = sums[:, h * LANES : (h + 1) * LANES]
        else:
            out_ref[h, hd:, :] = jnp.zeros((small.shape[0], rows), BF16)
    result.wait()


def backward_kernel(
    shares, d_mixed_in, gathered_ref, qkvt_in, v_in, soft_in, message_out,
    normed, d_query, d_key, d_value, joined, grad, qkvt_ref, v_ref, soft_ref, in_ref, out_ref,
    sems, fetch_sems, out_sems
):
    blocks, width = gathered_ref.shape[0], gathered_ref.shape[2]
    hd = v_ref.shape[1]
    total = blocks * WIN
    groups = sems.shape[0]
    per = blocks // groups
    copies = []
    for c in range(groups):
        low, high = (2 + c * per) * WIN * (c > 0), (2 + (c + 1) * per) * WIN
        window, own = pl.ds(low, high - low), pl.ds(c * per, per)
        copies.append([
            pltpu.make_async_copy(v_in.at[window], v_ref.at[window], sems.at[c, 0]),
            pltpu.make_async_copy(d_mixed_in.at[own], in_ref.at[own], sems.at[c, 1]),
            pltpu.make_async_copy(soft_in.at[own], soft_ref.at[own], sems.at[c, 2]),
            pltpu.make_async_copy(qkvt_in.at[:, window], qkvt_ref.at[:, window], sems.at[c, 3]),
        ])
    for group in copies:
        for copy in group:
            copy.start()
    steps = fetch_sems.shape[0]
    step = width // steps
    fetches = [
        pltpu.make_async_copy(
            gathered_ref.at[:, :, pl.ds(c * step, step)],
            normed.at[:, :, pl.ds(c * step, step)],
            fetch_sems.at[c],
        )
        for c in range(steps)
    ]
    d_key[...] = jnp.zeros(d_key.shape, F32)
    d_value[...] = jnp.zeros(d_value.shape, F32)
    scale = hd ** (-0.5)

    def attend(i, carry):
        start = pl.multiple_of(i * WIN, WIN)
        own = pl.ds(pl.multiple_of(start + WIN, WIN), WIN)
        window = pl.ds(start, 3 * WIN)
        d_mixed = in_ref[i, 0:hd, :]
        soft = soft_ref[i]
        wide = soft.astype(F32)
        d_soft = dot(v_ref[window, :], d_mixed, (1, 0))
        inner = jnp.sum(wide * d_soft, axis=0, keepdims=True)
        d_scores = (wide * (d_soft - inner) * scale).astype(BF16)
        d_query[:, pl.ds(start, WIN)] = dot(qkvt_ref[hd : 2 * hd, window], d_scores, (1, 0)).astype(BF16)
        d_key[:, window] += dot(qkvt_ref[0:hd, own], d_scores, (1, 1))
        d_value[:, window] += dot(d_mixed, soft, (1, 1))
        return carry

    for c, group in enumerate(copies):
        for copy in group:
            copy.wait()
        if c == 0:
            for fetch in fetches:
                fetch.start()
        lax.fori_loop(c * per, (c + 1) * per, attend, 0, unroll=True)
    joined[0:hd, :] = d_query[...]
    joined[hd : 2 * hd, :] = d_key[:, WIN : WIN + total].astype(BF16)
    joined[2 * hd :, :] = d_value[:, WIN : WIN + total].astype(BF16)
    rest = 3 * hd - 2 * LANES
    repeats = LANES // rest
    share = width // shares
    third = share // (repeats - 1)
    lane = lax.broadcasted_iota(jnp.int32, (1, LANES), 1) // rest
    each = step // share
    sends = []
    for c, fetch in enumerate(fetches):
        fetch.wait()
        rows = normed[:, :, c * step : (c + 1) * step].reshape(total, step)
        part = dot(joined[...], rows, (1, 0))
        tail = part[2 * LANES :]
        grad[c] = jnp.concatenate([part[: 2 * LANES]] + [tail] * repeats, axis=0).T
        for j in range(each):
            d = c * each + j
            at = slice(j * share, (j + 1) * share)
            out_ref[d, 0:share, :] = grad[c, at, 0:LANES].astype(BF16)
            out_ref[d, share : 2 * share, :] = grad[c, at, LANES : 2 * LANES].astype(BF16)
            packed = jnp.zeros((third, LANES), F32)
            for i in range(repeats - 1):
                first = j * share + i * third
                packed = jnp.where(lane == i, grad[c, first : first + third, 2 * LANES :], packed)
            out_ref[d, 2 * share :, :] = packed.astype(BF16)
        done = pl.ds(c * each, each)
        sends.append(pltpu.make_async_copy(out_ref.at[done], message_out.at[done], out_sems.at[c]))
        sends[-1].start()
    for send in sends:
        send.wait()


def sum_kernel(in_ref, grad_ref):
    share, columns = grad_ref.shape[0], grad_ref.shape[2]
    third = in_ref.shape[1] - 2 * share
    rest = columns - 2 * LANES
    summed = jnp.sum(in_ref[...].astype(F32), axis=0)
    grad_ref[:, 0, 0:LANES] = summed[0:share]
    grad_ref[:, 0, LANES : 2 * LANES] = summed[share : 2 * share]
    for j in range(share // third):
        grad_ref[j * third : (j + 1) * third, 0, 2 * LANES :] = summed[
            2 * share : 2 * share + third, j * rest : (j + 1) * rest
        ]


def spread_kernel(in_ref, kernel_ref, scale_ref, shift_ref):
    taps = kernel_ref.shape[0]
    for c in range(kernel_ref.shape[1] // LANES):
        at = slice(c * LANES, (c + 1) * LANES)
        kernel_ref[:, at] = in_ref[c, 0:taps, :]
        scale_ref[at] = in_ref[c, taps, :]
        shift_ref[at] = in_ref[c, taps + 1, :]


def on_device(frames, lengths, w_qkv, w_out, kernel, bn_scale, bn_shift, cotangent):
    blocks = lax.axis_size("seq")
    shares = lax.axis_size("dp")
    rows, width = frames.shape[1], frames.shape[2]
    hd = w_out.shape[1]
    total = rows * blocks
    taps = kernel.shape[0]
    small_rows = 16
    shape = jax.ShapeDtypeStruct
    x, g = frames[0], cotangent[0]

    with jax.named_scope("norm"):
        normed = pl.pallas_call(
            norm_kernel,
            in_specs=[HBM],
            out_specs=HBM,
            out_shape=shape((rows, width), BF16),
            scratch_shapes=[
                pltpu.VMEM((rows, width), BF16),
                pltpu.VMEM((rows, width), BF16),
                pltpu.SemaphoreType.DMA((2, 2)),
            ],
            compiler_params=params(60),
        )(x)
    with jax.named_scope("gather"):
        gathered = lax.all_gather(normed, "seq")
    with jax.named_scope("halo"):
        upward = [(i, i + 1) for i in range(blocks - 1)]
        downward = [(j, i) for i, j in upward]
        tails = jnp.concatenate([x[rows - EDGE :], g[rows - EDGE :]], axis=0)
        heads = jnp.concatenate([x[:EDGE], g[:EDGE]], axis=0)
        before = lax.ppermute(tails, "seq", upward)
        after = lax.ppermute(heads, "seq", downward)
    firsts = 4
    per = shares // firsts
    chunk = width // firsts
    with jax.named_scope("w_out_columns"):
        quarter = lax.dynamic_slice_in_dim(
            w_out, lax.axis_index("dp") // per * chunk, chunk, axis=2
        )
        same = [list(range(c, blocks, 2)) for c in range(2)]
        twins = [(i, i ^ 1) for i in range(blocks)]
        columns = jnp.broadcast_to(quarter, (blocks // 2, hd, chunk))
        columns = lax.all_to_all(columns, "seq", 0, 0, axis_index_groups=same)
        columns = jnp.concatenate([columns, lax.ppermute(columns, "seq", twins)], axis=0)
        def onward(dp, seq):
            first = (dp // per + 1 - 2 * (seq % 2)) % firsts
            return (first * per + dp % per) * blocks + seq

        ring = [(d * blocks + i, onward(d, i)) for d in range(shares) for i in range(blocks)]
        near = lax.ppermute(columns, ("dp", "seq"), ring)
        place = jnp.stack([lax.axis_index("seq"), lengths[0], lax.axis_index("dp") // per])
        gain, offset = bn_scale.reshape(1, width), bn_shift.reshape(1, width)
        near, before, after, place, gain, offset = lax.optimization_barrier(
            (near, before, after, place, gain, offset)
        )
        twin = lax.ppermute(near, "seq", twins)
        far = lax.ppermute(near, ("dp", "seq"), ring)
    gathered, near = lax.optimization_barrier((gathered, near))
    wt = w_qkv.reshape(width, 3 * hd).T

    with jax.named_scope("forward"):
        mixed, qkvt, v, soft = pl.pallas_call(
            forward_kernel,
            in_specs=[SMEM, HBM, VMEM],
            out_specs=[VMEM] + [HBM] * 3,
            out_shape=[
                shape((blocks, hd + 2 * EDGE, WIN), BF16),
                shape((3 * hd, total + 2 * WIN), BF16),
                shape((total + 2 * WIN, hd), BF16),
                shape((blocks, 3 * WIN, WIN), BF16),
            ],
            scratch_shapes=[
                pltpu.VMEM((blocks, WIN, width), BF16),
                pltpu.VMEM((blocks + 2, LANES, WIN), F32),
                pltpu.VMEM((3 * hd, total + 2 * WIN), BF16),
                pltpu.VMEM((total + 2 * WIN, LANES), BF16),
                pltpu.VMEM((total + 2 * WIN, hd), BF16),
                pltpu.VMEM((blocks, 3 * WIN, WIN), BF16),
                pltpu.VMEM((3 * WIN, WIN), F32),
                pltpu.SemaphoreType.DMA((4,)),
                pltpu.SemaphoreType.DMA((12,)),
            ],
            compiler_params=params(54),
        )(lengths, gathered, wt)
    mixed, twin, far = lax.optimization_barrier((mixed, twin, far))
    with jax.named_scope("mixed_exchange"):
        mixed = lax.all_to_all(mixed, "seq", 0, 0)

    with jax.named_scope("middle"):
        layer_out, d_mixed = pl.pallas_call(
            functools.partial(middle_kernel, total),
            in_specs=[SMEM] + [HBM] * 9 + [VMEM] * 3,
            out_specs=[HBM, VMEM],
            out_shape=[
                shape((rows, width), BF16),
                shape((blocks, hd + small_rows, rows), BF16),
            ],
            scratch_shapes=[
                pltpu.VMEM(mixed.shape, BF16),
                pltpu.VMEM((rows, width), BF16),
                pltpu.VMEM((rows, width), BF16),
                pltpu.VMEM((2 * EDGE, width), BF16),
                pltpu.VMEM((2 * EDGE, width), BF16),
                pltpu.VMEM((rows, width), BF16),
                pltpu.VMEM((firsts, blocks, hd, chunk), BF16),
                pltpu.VMEM((rows, width), BF16),
                pltpu.VMEM((rows + 2 * EDGE + taps - 1, chunk), F32),
                pltpu.VMEM((rows + 2 * EDGE, chunk), F32),
                pltpu.VMEM((small_rows, width), F32),
                pltpu.SemaphoreType.DMA((firsts, 2)),
                pltpu.SemaphoreType.DMA((6,)),
            ],
            compiler_params=params(30),
        )(
            place, mixed, x, g, before, after, columns, near, twin, far, kernel, gain, offset,
        )
    with jax.named_scope("d_mixed_exchange"):
        d_mixed = lax.all_to_all(d_mixed, "seq", 0, 0)

    share = width // shares
    third = LANES // 8
    across = [[i * per + j for i in range(firsts)] for j in range(per)]
    along = [[i * per + j for j in range(per)] for i in range(firsts)]
    with jax.named_scope("small_sums"):
        small = jnp.sum(d_mixed[:, hd:].astype(F32), axis=0)
        small = lax.all_to_all(
            jnp.broadcast_to(small, (per,) + small.shape), "dp", 0, 0, axis_index_groups=along
        )
    with jax.named_scope("backward"):
        messages = pl.pallas_call(
            functools.partial(backward_kernel, shares),
            in_specs=[HBM] * 5,
            out_specs=HBM,
            out_shape=shape((shares, 2 * share + third, LANES), BF16),
            scratch_shapes=[
                pltpu.VMEM((blocks, WIN, width), BF16),
                pltpu.VMEM((hd, total), BF16),
                pltpu.VMEM((hd, total + 2 * WIN), F32),
                pltpu.VMEM((hd, total + 2 * WIN), F32),
                pltpu.VMEM((3 * hd, total), BF16),
                pltpu.VMEM((4, width // 4, 3 * LANES), F32),
                pltpu.VMEM((3 * hd, total + 2 * WIN), BF16),
                pltpu.VMEM((total + 2 * WIN, hd), BF16),
                pltpu.VMEM((blocks, 3 * WIN, WIN), BF16),
                pltpu.VMEM((blocks, hd + small_rows, WIN), BF16),
                pltpu.VMEM((shares, 2 * share + third, LANES), BF16),
                pltpu.SemaphoreType.DMA((4, 4)),
                pltpu.SemaphoreType.DMA((4,)),
                pltpu.SemaphoreType.DMA((4,)),
            ],
            compiler_params=params(56),
        )(d_mixed, gathered, qkvt, v, soft)
    messages, small = lax.optimization_barrier((messages, small))
    with jax.named_scope("grad_exchange"):
        messages = lax.all_to_all(messages, "dp", 0, 0)
    with jax.named_scope("small_gathers"):
        small = jnp.sum(small, axis=0)
        small = jnp.sum(lax.all_gather(small, "dp", axis_index_groups=across), axis=0)
        small = lax.all_gather(small, "seq")
    with jax.named_scope("sum"):
        grad_qkv = pl.pallas_call(
            sum_kernel,
            in_specs=[VMEM],
            out_specs=VMEM,
            out_shape=shape((share, 1, 3 * hd), F32),
            compiler_params=params(16),
        )(messages)
    with jax.named_scope("spread"):
        grad_kernel, grad_scale, grad_shift = pl.pallas_call(
            spread_kernel,
            in_specs=[VMEM],
            out_specs=[VMEM] * 3,
            out_shape=[shape((taps, width), F32), shape((width,), F32), shape((width,), F32)],
            compiler_params=params(16),
        )(small)
    return (
        layer_out[None],
        grad_qkv,
        grad_kernel,
        grad_scale,
        grad_shift,
    )


def solution(mesh):
    in_specs = (
        P("dp", "seq", None),
        P("dp"),
        P(None, "seq", None),
        P("seq", None, None),
        P(),
        P(),
        P(),
        P("dp", "seq", None),
    )
    out_specs = (P("dp", "seq", None), P("dp", "seq", None), P(), P(), P())
    return jax.shard_map(
        on_device, mesh=mesh, in_specs=in_specs, out_specs=out_specs, check_vma=False
    )
```

```python
import functools

import jax
import jax.numpy as jnp
from jax import lax
from jax.experimental import pallas as pl
from jax.experimental.pallas import tpu as pltpu
from jax.sharding import PartitionSpec as P

WIN = 128
EPS = 1e-05
FLOOR = 1.0
FAR = -1e30
EDGE = 8
LANES = 128
F32 = jnp.float32
BF16 = jnp.bfloat16

VMEM = pl.BlockSpec(memory_space=pltpu.VMEM)
SMEM = pl.BlockSpec(memory_space=pltpu.SMEM)
HBM = pl.BlockSpec(memory_space=pltpu.HBM)


def params(mib):
    return pltpu.CompilerParams(vmem_limit_bytes=mib * 1024 * 1024)


def dot(a, b, dims):
    return lax.dot_general(a, b, ((dims[:1], dims[1:]), ((), ())), preferred_element_type=F32)


def norm_kernel(x_in, normed_out, x_ref, normed_ref, sems):
    parts = sems.shape[1]
    step = x_ref.shape[0] // parts
    places = [pl.ds(c * step, step) for c in range(parts)]
    takes = [
        pltpu.make_async_copy(x_in.at[at], x_ref.at[at], sems.at[0, c])
        for c, at in enumerate(places)
    ]
    gives = [
        pltpu.make_async_copy(normed_ref.at[at], normed_out.at[at], sems.at[1, c])
        for c, at in enumerate(places)
    ]
    for take in takes:
        take.start()
    for at, take, give in zip(places, takes, gives):
        take.wait()
        values = x_ref[at, :].astype(F32)
        center = values - jnp.mean(values, axis=-1, keepdims=True)
        spread = jnp.mean(center * center, axis=-1, keepdims=True)
        normed_ref[at, :] = (center * lax.rsqrt(spread + EPS)).astype(BF16)
        give.start()
    for give in gives:
        give.wait()


def forward_kernel(
    len_ref, gathered_ref, wt_ref, out_ref, qkvt_out, v_out, soft_out,
    normed, mixed, qkvt_ref, k_ref, v_ref, soft_ref, bias, sems, out_sems
):
    blocks = gathered_ref.shape[0]
    hd = v_ref.shape[1]
    total = blocks * WIN
    per = blocks // sems.shape[0]
    sends = []

    def send(source, target):
        sends.append(pltpu.make_async_copy(source, target, out_sems.at[len(sends)]))
        sends[-1].start()

    copies = [
        pltpu.make_async_copy(
            gathered_ref.at[pl.ds(c * per, per)],
            normed.at[pl.ds(c * per, per)],
            sems.at[c],
        )
        for c in range(sems.shape[0])
    ]
    for copy in copies:
        copy.start()
    length = len_ref[0]
    key = lax.broadcasted_iota(jnp.int32, (3 * WIN, WIN), 0)
    query = lax.broadcasted_iota(jnp.int32, (3 * WIN, WIN), 1)
    near = (key >= query) & (key - query <= 2 * WIN)
    bias[...] = jnp.where(near, 0.0, FAR)
    extra = k_ref.shape[1] - hd
    position = lax.broadcasted_iota(jnp.int32, (total + 2 * WIN, extra), 0) - WIN
    dead = (position < 0) | (position >= length)
    k_ref[:, hd:] = jnp.where(dead, FAR, 0.0).astype(BF16)
    ones = (lax.broadcasted_iota(jnp.int32, (extra, WIN), 0) == 0).astype(F32).astype(BF16)
    for edge in (slice(0, WIN), slice(WIN + total, 2 * WIN + total)):
        qkvt_ref[:, edge] = jnp.zeros((3 * hd, WIN), BF16)
        k_ref[edge, 0:hd] = jnp.zeros((WIN, hd), BF16)
        v_ref[edge, :] = jnp.zeros((WIN, hd), BF16)
    mixed[0] = jnp.zeros(mixed.shape[1:], F32)
    mixed[blocks + 1] = jnp.zeros(mixed.shape[1:], F32)
    column = lax.broadcasted_iota(jnp.int32, (1, WIN), 1)
    scale = hd ** (-0.5)

    def attend(i, carry):
        start = pl.multiple_of(i * WIN, WIN)
        q = qkvt_ref[0:hd, pl.ds(pl.multiple_of(start + WIN, WIN), WIN)]
        q = jnp.concatenate([q, ones], axis=0)
        scores = dot(k_ref[pl.ds(start, 3 * WIN), :], q, (1, 0)) * scale + bias[...]
        top = jnp.max(scores, axis=0, keepdims=True)
        expo = jnp.exp(scores - top)
        denominator = jnp.maximum(jnp.sum(expo, axis=0, keepdims=True), FLOOR)
        soft = (expo * (1.0 / denominator)).astype(BF16)
        soft_ref[i] = soft
        result = dot(qkvt_ref[2 * hd : 3 * hd, pl.ds(start, 3 * WIN)], soft, (1, 0))
        result = jnp.where(column + start < length, result, 0.0)
        mixed[i + 1, 0:hd, :] = result
        mixed[i + 1, hd:, :] = jnp.zeros((mixed.shape[1] - hd, WIN), F32)
        out_ref[i, 0:hd, :] = result.astype(BF16)
        return carry

    wt = wt_ref[...]

    def project(c, carry):
        here = pl.ds(c * per, per)
        pltpu.make_async_copy(gathered_ref.at[here], normed.at[here], sems.at[c]).wait()
        rows = normed[here].reshape(per * WIN, normed.shape[2])
        part = dot(wt, rows, (1, 1))
        at = pl.ds(pl.multiple_of((1 + c * per) * WIN, WIN), per * WIN)
        qkvt_ref[:, at] = part.astype(BF16)
        k_ref[at, 0:hd] = part[hd : 2 * hd].T.astype(BF16)
        v_ref[at, :] = part[2 * hd :].T.astype(BF16)
        return carry

    lax.fori_loop(0, len(copies), project, 0)
    send(qkvt_ref, qkvt_out)
    send(v_ref, v_out)

    def save(c):
        here = pl.ds(c * per, per)
        return pltpu.make_async_copy(soft_ref.at[here], soft_out.at[here], out_sems.at[2 + c])

    def attend_group(c, carry):
        for j in range(per):
            attend(c * per + j, carry)
        save(c).start()
        return carry

    lax.fori_loop(0, len(copies), attend_group, 0)

    def edges(i, carry):
        both = jnp.where(column < EDGE, mixed[i + 2], mixed[i]).T
        rows = jnp.concatenate([both[WIN - EDGE :], both[:EDGE]], axis=0)
        out_ref[i, hd:, :] = rows.astype(BF16)
        return carry

    lax.fori_loop(0, blocks, edges, 0, unroll=4)
    for copy in sends + [save(c) for c in range(len(copies))]:
        copy.wait()


def middle_kernel(
    total, place_ref, mix_in, x_in, g_in, prev_in, next_in, own_ref, near_ref, twin_ref, far_ref,
    taps_ref, scale_ref, shift_ref, layer_out, out_ref, mix_ref, x_ref, g_ref,
    prev_ref, next_ref, layer_ref, weight, d_hidden, masked, d_conv, small, sems, more_sems
):
    inputs = [
        pltpu.make_async_copy(source, target, more_sems.at[i])
        for i, (source, target) in enumerate((
            (mix_in, mix_ref), (prev_in, prev_ref), (next_in, next_ref), (x_in, x_ref),
            (g_in, g_ref),
        ))
    ]
    for copy in inputs:
        copy.start()
    heads, width = mix_ref.shape[0], x_ref.shape[1]
    rows = x_ref.shape[0]
    quarters, _, hd, chunk = weight.shape
    core = lax.rem(place_ref[0], 2)
    half = heads // 2
    first, last = pl.ds(0, half), pl.ds(half, half)
    pieces = (
        (0, own_ref.at[first], own_ref.at[last]),
        (2 * core - 1, near_ref.at[first], near_ref.at[last]),
        (1 - 2 * core, twin_ref.at[last], twin_ref.at[first]),
        (2, far_ref.at[first], far_ref.at[last]),
    )

    def fetch(quarter, lower, upper):
        for j, piece in enumerate((lower, upper)):
            target = weight.at[quarter, pl.ds(j * half, half)]
            pltpu.make_async_copy(piece, target, sems.at[quarter, j]).start()

    for quarter in range(quarters):
        for step, lower, upper in pieces:
            holds = lax.rem(place_ref[2] + step + quarters, quarters) == quarter
            pl.when(holds)(functools.partial(fetch, quarter, lower, upper))
    taps_count = taps_ref.shape[0]
    reach = (taps_count - 1) // 2
    ext = rows + 2 * EDGE
    length = place_ref[1]
    base = place_ref[0] * rows
    order = [core + 2 * j for j in range(heads // 2)] + [1 - core + 2 * j for j in range(heads // 2)]
    inputs[0].wait()
    body = jnp.concatenate([mix_ref[h, 0:hd, :] for h in order], axis=0).T
    fringe = jnp.concatenate([mix_ref[h, hd:, 0:hd] for h in order], axis=1)
    mix = jnp.concatenate([body, fringe], axis=0)
    pos = lax.broadcasted_iota(jnp.int32, (ext, 1), 0) + (base - EDGE)
    live = (pos >= 0) & (pos < length)
    inside = (pos >= 0) & (pos < total)
    live_here = live[EDGE : EDGE + rows]
    small[...] = jnp.zeros(small.shape, F32)
    masked[0:reach, :] = jnp.zeros((reach, chunk), F32)
    masked[reach + ext :, :] = jnp.zeros((reach, chunk), F32)
    for copy in inputs[1:]:
        copy.wait()
    for c in range(quarters):
        at = slice(c * chunk, (c + 1) * chunk)
        for j in range(2):
            target = weight.at[c, pl.ds(j * half, half)]
            pltpu.make_async_copy(target, target, sems.at[c, j]).wait()
        w = weight[c].reshape(heads * hd, chunk)
        attended = dot(mix, w, (1, 0))
        attended = jnp.concatenate(
            [attended[rows : rows + EDGE], attended[:rows], attended[rows + EDGE :]], axis=0
        )
        before = prev_ref[:, at].astype(F32)
        after = next_ref[:, at].astype(F32)
        frames = jnp.concatenate([before[:EDGE], x_ref[:, at].astype(F32), after[:EDGE]], axis=0)
        upstream = jnp.concatenate([before[EDGE:], g_ref[:, at].astype(F32), after[EDGE:]], axis=0)
        hidden = (frames + attended).astype(BF16).astype(F32)
        masked[reach : reach + ext, :] = jnp.where(live, hidden, 0.0)
        taps = taps_ref[:, at].astype(F32)
        conv = jnp.zeros((ext, chunk), F32)
        for k in range(taps_count):
            conv = conv + masked[k : k + ext, :] * taps[k : k + 1]
        gain = scale_ref[:, at]
        shifted = conv * gain + shift_ref[:, at]
        sigmoid = jax.nn.sigmoid(shifted)
        d_shifted = upstream * sigmoid * (1.0 + shifted * (1.0 - sigmoid))
        own = slice(EDGE, EDGE + rows)
        layer_ref[:, at] = (hidden[own] + (shifted * sigmoid)[own]).astype(BF16)
        d_own = d_shifted[own]
        small[taps_count : taps_count + 1, at] = jnp.sum(d_own * conv[own], axis=0, keepdims=True)
        small[taps_count + 1 : taps_count + 2, at] = jnp.sum(d_own, axis=0, keepdims=True)
        d_conv[...] = jnp.where(inside, d_shifted * gain, 0.0)
        d_conv_own = d_own * gain
        spread = jnp.zeros((rows, chunk), F32)
        for k in range(taps_count):
            small[k : k + 1, at] = jnp.sum(
                d_conv_own * masked[EDGE + k : EDGE + k + rows, :], axis=0, keepdims=True
            )
            first = EDGE + reach - k
            spread = spread + taps[k : k + 1] * d_conv[first : first + rows, :]
        d_hidden[:, at] = (upstream[own] + jnp.where(live_here, spread, 0.0)).astype(BF16)
    result = pltpu.make_async_copy(layer_ref, layer_out, more_sems.at[len(inputs)])
    result.start()
    column = lax.broadcasted_iota(jnp.int32, (1, rows), 1) + base
    group = 4
    for h in range(0, heads, group):
        d_mixed = jnp.zeros((group * hd, rows), F32)
        for c in range(quarters):
            w = weight[c, h : h + group].reshape(group * hd, chunk)
            d_mixed = d_mixed + dot(w, d_hidden[:, c * chunk : (c + 1) * chunk], (1, 1))
        d_mixed = jnp.where(column < length, d_mixed, 0.0).astype(BF16)
        for j in range(group):
            out_ref[order[h + j], 0:hd, :] = d_mixed[j * hd : (j + 1) * hd]
    sums = small[...].astype(BF16)
    for h in range(heads):
        if (h + 1) * LANES <= width:
            out_ref[h, hd:, :] = sums[:, h * LANES : (h + 1) * LANES]
        else:
            out_ref[h, hd:, :] = jnp.zeros((small.shape[0], rows), BF16)
    result.wait()


def backward_kernel(
    shares, d_mixed_in, gathered_ref, qkvt_in, v_in, soft_in, message_out,
    normed, d_query, d_key, d_value, joined, grad, qkvt_ref, v_ref, soft_ref, in_ref, out_ref,
    sems, fetch_sems, out_sems
):
    blocks, width = gathered_ref.shape[0], gathered_ref.shape[2]
    hd = v_ref.shape[1]
    total = blocks * WIN
    groups = sems.shape[0] - 1
    per = blocks // groups
    lead = pl.ds(0, 2 * WIN)
    ahead = [
        pltpu.make_async_copy(v_in.at[lead], v_ref.at[lead], sems.at[groups, 0]),
        pltpu.make_async_copy(qkvt_in.at[:, lead], qkvt_ref.at[:, lead], sems.at[groups, 1]),
    ]

    def group_copies(c):
        window = pl.ds(pl.multiple_of((2 + c * per) * WIN, WIN), per * WIN)
        own = pl.ds(c * per, per)
        return [
            pltpu.make_async_copy(v_in.at[window], v_ref.at[window], sems.at[c, 0]),
            pltpu.make_async_copy(d_mixed_in.at[own], in_ref.at[own], sems.at[c, 1]),
            pltpu.make_async_copy(soft_in.at[own], soft_ref.at[own], sems.at[c, 2]),
            pltpu.make_async_copy(qkvt_in.at[:, window], qkvt_ref.at[:, window], sems.at[c, 3]),
        ]

    for copy in ahead:
        copy.start()
    for c in range(groups):
        for copy in group_copies(c):
            copy.start()
    steps = fetch_sems.shape[0]
    step = width // steps
    fetches = [
        pltpu.make_async_copy(
            gathered_ref.at[:, :, pl.ds(c * step, step)],
            normed.at[:, :, pl.ds(c * step, step)],
            fetch_sems.at[c],
        )
        for c in range(steps)
    ]
    d_key[...] = jnp.zeros(d_key.shape, F32)
    d_value[...] = jnp.zeros(d_value.shape, F32)
    scale = hd ** (-0.5)

    def attend(i, carry):
        start = pl.multiple_of(i * WIN, WIN)
        own = pl.ds(pl.multiple_of(start + WIN, WIN), WIN)
        window = pl.ds(start, 3 * WIN)
        d_mixed = in_ref[i, 0:hd, :]
        soft = soft_ref[i]
        wide = soft.astype(F32)
        d_soft = dot(v_ref[window, :], d_mixed, (1, 0))
        inner = jnp.sum(wide * d_soft, axis=0, keepdims=True)
        d_scores = (wide * (d_soft - inner) * scale).astype(BF16)
        d_query[:, pl.ds(start, WIN)] = dot(qkvt_ref[hd : 2 * hd, window], d_scores, (1, 0)).astype(BF16)
        d_key[:, window] += dot(qkvt_ref[0:hd, own], d_scores, (1, 1))
        d_value[:, window] += dot(d_mixed, soft, (1, 1))
        return carry

    for fetch in fetches:
        fetch.start()
    for copy in ahead:
        copy.wait()

    def attend_group(c, carry):
        for copy in group_copies(c):
            copy.wait()
        for j in range(per):
            attend(c * per + j, carry)
        return carry

    lax.fori_loop(0, groups, attend_group, 0)
    joined[0:hd, :] = d_query[...]
    joined[hd : 2 * hd, :] = d_key[:, WIN : WIN + total].astype(BF16)
    joined[2 * hd :, :] = d_value[:, WIN : WIN + total].astype(BF16)
    rest = 3 * hd - 2 * LANES
    repeats = LANES // rest
    share = width // shares
    third = share // (repeats - 1)
    lane = lax.broadcasted_iota(jnp.int32, (1, LANES), 1) // rest
    each = step // share

    def send(c):
        done = pl.ds(c * each, each)
        return pltpu.make_async_copy(out_ref.at[done], message_out.at[done], out_sems.at[c])

    def gradient(c, carry):
        columns = pl.ds(pl.multiple_of(c * step, LANES), step)
        pltpu.make_async_copy(
            gathered_ref.at[:, :, columns], normed.at[:, :, columns], fetch_sems.at[c]
        ).wait()
        part = dot(joined[...], normed[:, :, columns].reshape(total, step), (1, 0))
        tail = part[2 * LANES :]
        grad[...] = jnp.concatenate([part[: 2 * LANES]] + [tail] * repeats, axis=0).T
        for j in range(each):
            d = c * each + j
            at = slice(j * share, (j + 1) * share)
            out_ref[d, 0:share, :] = grad[at, 0:LANES].astype(BF16)
            out_ref[d, share : 2 * share, :] = grad[at, LANES : 2 * LANES].astype(BF16)
            packed = jnp.zeros((third, LANES), F32)
            for i in range(repeats - 1):
                first = j * share + i * third
                packed = jnp.where(lane == i, grad[first : first + third, 2 * LANES :], packed)
            out_ref[d, 2 * share :, :] = packed.astype(BF16)
        send(c).start()
        return carry

    lax.fori_loop(0, steps, gradient, 0)
    for c in range(steps):
        send(c).wait()


def sum_kernel(in_ref, grad_ref):
    share, columns = grad_ref.shape[0], grad_ref.shape[2]
    third = in_ref.shape[1] - 2 * share
    rest = columns - 2 * LANES
    summed = jnp.sum(in_ref[...].astype(F32), axis=0)
    grad_ref[:, 0, 0:LANES] = summed[0:share]
    grad_ref[:, 0, LANES : 2 * LANES] = summed[share : 2 * share]
    for j in range(share // third):
        grad_ref[j * third : (j + 1) * third, 0, 2 * LANES :] = summed[
            2 * share : 2 * share + third, j * rest : (j + 1) * rest
        ]


def spread_kernel(in_ref, kernel_ref, scale_ref, shift_ref):
    taps = kernel_ref.shape[0]
    for c in range(kernel_ref.shape[1] // LANES):
        at = slice(c * LANES, (c + 1) * LANES)
        kernel_ref[:, at] = in_ref[c, 0:taps, :]
        scale_ref[at] = in_ref[c, taps, :]
        shift_ref[at] = in_ref[c, taps + 1, :]


def on_device(frames, lengths, w_qkv, w_out, kernel, bn_scale, bn_shift, cotangent):
    blocks = lax.axis_size("seq")
    shares = lax.axis_size("dp")
    rows, width = frames.shape[1], frames.shape[2]
    hd = w_out.shape[1]
    total = rows * blocks
    taps = kernel.shape[0]
    small_rows = 16
    shape = jax.ShapeDtypeStruct
    x, g = frames[0], cotangent[0]

    with jax.named_scope("norm"):
        normed = pl.pallas_call(
            norm_kernel,
            in_specs=[HBM],
            out_specs=HBM,
            out_shape=shape((rows, width), BF16),
            scratch_shapes=[
                pltpu.VMEM((rows, width), BF16),
                pltpu.VMEM((rows, width), BF16),
                pltpu.SemaphoreType.DMA((2, 2)),
            ],
            compiler_params=params(60),
        )(x)
    with jax.named_scope("gather"):
        gathered = lax.all_gather(normed, "seq")
    with jax.named_scope("halo"):
        upward = [(i, i + 1) for i in range(blocks - 1)]
        downward = [(j, i) for i, j in upward]
        tails = jnp.concatenate([x[rows - EDGE :], g[rows - EDGE :]], axis=0)
        heads = jnp.concatenate([x[:EDGE], g[:EDGE]], axis=0)
        before = lax.ppermute(tails, "seq", upward)
        after = lax.ppermute(heads, "seq", downward)
    firsts = 4
    per = shares // firsts
    chunk = width // firsts
    with jax.named_scope("w_out_columns"):
        quarter = lax.dynamic_slice_in_dim(
            w_out, lax.axis_index("dp") // per * chunk, chunk, axis=2
        )
        same = [list(range(c, blocks, 2)) for c in range(2)]
        twins = [(i, i ^ 1) for i in range(blocks)]
        columns = jnp.broadcast_to(quarter, (blocks // 2, hd, chunk))
        columns = lax.all_to_all(columns, "seq", 0, 0, axis_index_groups=same)
        columns = jnp.concatenate([columns, lax.ppermute(columns, "seq", twins)], axis=0)
        def onward(dp, seq):
            first = (dp // per + 1 - 2 * (seq % 2)) % firsts
            return (first * per + dp % per) * blocks + seq

        ring = [(d * blocks + i, onward(d, i)) for d in range(shares) for i in range(blocks)]
        near = lax.ppermute(columns, ("dp", "seq"), ring)
        place = jnp.stack([lax.axis_index("seq"), lengths[0], lax.axis_index("dp") // per])
        gain, offset = bn_scale.reshape(1, width), bn_shift.reshape(1, width)
        near, before, after, place, gain, offset = lax.optimization_barrier(
            (near, before, after, place, gain, offset)
        )
        twin = lax.ppermute(near, "seq", twins)
        far = lax.ppermute(near, ("dp", "seq"), ring)
    gathered, near = lax.optimization_barrier((gathered, near))
    wt = w_qkv.reshape(width, 3 * hd).T

    with jax.named_scope("forward"):
        mixed, qkvt, v, soft = pl.pallas_call(
            forward_kernel,
            in_specs=[SMEM, HBM, VMEM],
            out_specs=[VMEM] + [HBM] * 3,
            out_shape=[
                shape((blocks, hd + 2 * EDGE, WIN), BF16),
                shape((3 * hd, total + 2 * WIN), BF16),
                shape((total + 2 * WIN, hd), BF16),
                shape((blocks, 3 * WIN, WIN), BF16),
            ],
            scratch_shapes=[
                pltpu.VMEM((blocks, WIN, width), BF16),
                pltpu.VMEM((blocks + 2, LANES, WIN), F32),
                pltpu.VMEM((3 * hd, total + 2 * WIN), BF16),
                pltpu.VMEM((total + 2 * WIN, LANES), BF16),
                pltpu.VMEM((total + 2 * WIN, hd), BF16),
                pltpu.VMEM((blocks, 3 * WIN, WIN), BF16),
                pltpu.VMEM((3 * WIN, WIN), F32),
                pltpu.SemaphoreType.DMA((4,)),
                pltpu.SemaphoreType.DMA((6,)),
            ],
            compiler_params=params(54),
        )(lengths, gathered, wt)
    mixed, twin, far = lax.optimization_barrier((mixed, twin, far))
    with jax.named_scope("mixed_exchange"):
        mixed = lax.all_to_all(mixed, "seq", 0, 0)

    with jax.named_scope("middle"):
        layer_out, d_mixed = pl.pallas_call(
            functools.partial(middle_kernel, total),
            in_specs=[SMEM] + [HBM] * 9 + [VMEM] * 3,
            out_specs=[HBM, VMEM],
            out_shape=[
                shape((rows, width), BF16),
                shape((blocks, hd + small_rows, rows), BF16),
            ],
            scratch_shapes=[
                pltpu.VMEM(mixed.shape, BF16),
                pltpu.VMEM((rows, width), BF16),
                pltpu.VMEM((rows, width), BF16),
                pltpu.VMEM((2 * EDGE, width), BF16),
                pltpu.VMEM((2 * EDGE, width), BF16),
                pltpu.VMEM((rows, width), BF16),
                pltpu.VMEM((firsts, blocks, hd, chunk), BF16),
                pltpu.VMEM((rows, width), BF16),
                pltpu.VMEM((rows + 2 * EDGE + taps - 1, chunk), F32),
                pltpu.VMEM((rows + 2 * EDGE, chunk), F32),
                pltpu.VMEM((small_rows, width), F32),
                pltpu.SemaphoreType.DMA((firsts, 2)),
                pltpu.SemaphoreType.DMA((6,)),
            ],
            compiler_params=params(30),
        )(
            place, mixed, x, g, before, after, columns, near, twin, far, kernel, gain, offset,
        )
    with jax.named_scope("d_mixed_exchange"):
        d_mixed = lax.all_to_all(d_mixed, "seq", 0, 0)

    share = width // shares
    third = LANES // 8
    across = [[i * per + j for i in range(firsts)] for j in range(per)]
    along = [[i * per + j for j in range(per)] for i in range(firsts)]
    with jax.named_scope("small_sums"):
        small = jnp.sum(d_mixed[:, hd:].astype(F32), axis=0)
        small = lax.all_to_all(
            jnp.broadcast_to(small, (per,) + small.shape), "dp", 0, 0, axis_index_groups=along
        )
    with jax.named_scope("backward"):
        messages = pl.pallas_call(
            functools.partial(backward_kernel, shares),
            in_specs=[HBM] * 5,
            out_specs=HBM,
            out_shape=shape((shares, 2 * share + third, LANES), BF16),
            scratch_shapes=[
                pltpu.VMEM((blocks, WIN, width), BF16),
                pltpu.VMEM((hd, total), BF16),
                pltpu.VMEM((hd, total + 2 * WIN), F32),
                pltpu.VMEM((hd, total + 2 * WIN), F32),
                pltpu.VMEM((3 * hd, total), BF16),
                pltpu.VMEM((width // 4, 3 * LANES), F32),
                pltpu.VMEM((3 * hd, total + 2 * WIN), BF16),
                pltpu.VMEM((total + 2 * WIN, hd), BF16),
                pltpu.VMEM((blocks, 3 * WIN, WIN), BF16),
                pltpu.VMEM((blocks, hd + small_rows, WIN), BF16),
                pltpu.VMEM((shares, 2 * share + third, LANES), BF16),
                pltpu.SemaphoreType.DMA((5, 4)),
                pltpu.SemaphoreType.DMA((4,)),
                pltpu.SemaphoreType.DMA((4,)),
            ],
            compiler_params=params(56),
        )(d_mixed, gathered, qkvt, v, soft)
    messages, small = lax.optimization_barrier((messages, small))
    with jax.named_scope("grad_exchange"):
        messages = lax.all_to_all(messages, "dp", 0, 0)
    with jax.named_scope("small_gathers"):
        small = jnp.sum(small, axis=0)
        small = jnp.sum(lax.all_gather(small, "dp", axis_index_groups=across), axis=0)
        small = lax.all_gather(small, "seq")
    with jax.named_scope("sum"):
        grad_qkv = pl.pallas_call(
            sum_kernel,
            in_specs=[VMEM],
            out_specs=VMEM,
            out_shape=shape((share, 1, 3 * hd), F32),
            compiler_params=params(16),
        )(messages)
    with jax.named_scope("spread"):
        grad_kernel, grad_scale, grad_shift = pl.pallas_call(
            spread_kernel,
            in_specs=[VMEM],
            out_specs=[VMEM] * 3,
            out_shape=[shape((taps, width), F32), shape((width,), F32), shape((width,), F32)],
            compiler_params=params(16),
        )(small)
    return (
        layer_out[None],
        grad_qkv,
        grad_kernel,
        grad_scale,
        grad_shift,
    )


def solution(mesh):
    in_specs = (
        P("dp", "seq", None),
        P("dp"),
        P(None, "seq", None),
        P("seq", None, None),
        P(),
        P(),
        P(),
        P("dp", "seq", None),
    )
    out_specs = (P("dp", "seq", None), P("dp", "seq", None), P(), P(), P())
    return jax.shard_map(
        on_device, mesh=mesh, in_specs=in_specs, out_specs=out_specs, check_vma=False
    )
```
